32 devices in a mesh: gx: 8 (over z, y), gy: 4 (over x, core).
Axes of the slice: x: 2, y: 2, z: 4, core: 2. Of those that a mesh axis runs over, the one named last changes fastest.
Arguments:
- tokens: bfloat16 [128, 9216], P(('gx', 'gy')), may hold values from -6 to 6
- gain: float32 [9216], replicated, may hold values from 0.1 to 1.9
- w_gate: bfloat16 [9216, 36864], P('gy', 'gx'), may hold values from -0.0625 to 0.0625
- w_up: bfloat16 [9216, 36864], P('gy', 'gx'), may hold values from -0.0625 to 0.0625
- w_down: bfloat16 [36864, 9216], P('gx', 'gy'), may hold values from -0.03125 to 0.03125
- w_kv: bfloat16 [4, 2304, 512], P('gy', 'gx'), may hold values from -0.0625 to 0.0625
- queries: bfloat16 [128, 12288], P(('gx', 'gy')), may hold values from -64 to 64
- key_cache: bfloat16 [128, 2048, 256], P(('gx', 'gy')), may hold values from -4 to 4
- value_cache: bfloat16 [128, 2048, 256], P(('gx', 'gy')), may hold values from -6 to 6
- lengths: int32 [128], P(('gx', 'gy')), may hold values from 2 to 2048, as said below
Outputs:
- mixed: bfloat16 [128, 9216], P(('gx', 'gy'))
- context: bfloat16 [128, 12288], P(('gx', 'gy'))
The draws below stay inside these ranges and needn't reach their ends.
Inputs may be any that keep to these rules, and one draw needn't show every extreme that they name: `lengths`: each row has at least two live slots, and some row fills all 2048 slots.
All inputs are finite; a program needn't handle non-finite values.
Results may differ from the reference program's by a relative error of at most 0.0055.
Values may be sent and summed in bfloat16 or wider, within the bound.
No kernel may reach another device: no remote copies, remote signals or barrier semaphores. Data moves between devices by JAX's collectives and lax.ppermute only.
A program may use at most 128 MiB of HBM per device.

```python
import jax
import jax.numpy as jnp
from jax import lax

D = 9216
FF = 36864
HEADS = 48
HD = 256
CTX = 2048
ROWS = 128
N_GY = 4


def cache_keys(key):
    return jnp.clip(jax.random.normal(jax.random.fold_in(key, 11), (ROWS, CTX, HD), jnp.float32), -4.0, 4.0)


def draw_key_cache(key, part):
    keys = cache_keys(key)
    return keys.astype(jnp.bfloat16)


def draw_queries(key, part):
    drawn = jnp.clip(jax.random.normal(jax.random.fold_in(key, 15), (ROWS, HEADS, HD), jnp.float32), -4.0, 4.0)
    return drawn.reshape(ROWS, HEADS * HD).astype(jnp.bfloat16)


def draw_lengths(key, part):
    base = jax.random.randint(jax.random.fold_in(key, 17), (ROWS,), 2, CTX + 1)
    filled = jax.random.randint(jax.random.fold_in(key, 18), (), 0, ROWS)
    return jnp.where(jnp.arange(ROWS) == filled, CTX, base).astype(jnp.int32)


def block_scale(own_key, shape, pieces, low, top_value):
    level = 1.0
    for axis_at, shards_of in pieces:
        heights = jax.random.uniform(jax.random.fold_in(jax.random.fold_in(own_key, 6), axis_at), (shards_of,), jnp.float32, low / len(pieces), top_value / len(pieces))
        level = level * jnp.repeat(jnp.exp(heights), shape[axis_at] // shards_of).reshape((-1,) + (1,) * (len(shape) - 1 - axis_at))
    return level


def scatter_about(own_key, dims, scale, bound, cuts=(), dtype=jnp.bfloat16):
    loudness = block_scale(own_key, dims, cuts, -0.22, 0.18) if cuts else 1.0
    entries = jax.random.normal(own_key, dims, jnp.float32) * scale * loudness
    return jnp.minimum(jnp.maximum(entries, -bound), bound).astype(dtype)


def setup_inputs(seed: int = 0) -> dict:
    key_list = jax.random.split(jax.random.key(seed), 11)
    return {
        "tokens": scatter_about(key_list[0], (ROWS, D), 1.0, 6.0, ((0, 32),)),
        "gain": jnp.clip(1.0 + 0.18 * jax.random.normal(key_list[1], (D,), jnp.float32), 0.1, 1.9),
        "w_gate": scatter_about(key_list[2], (D, FF), D ** -0.5, 0.0625, ((0, 4), (1, 8))),
        "w_up": scatter_about(key_list[3], (D, FF), D ** -0.5, 0.0625, ((0, 4), (1, 8))),
        "w_down": scatter_about(key_list[4], (FF, D), FF ** -0.5, 0.03125, ((0, 8), (1, 4))),
        "w_kv": scatter_about(key_list[5], (N_GY, D // N_GY, 2 * HD), D ** -0.5, 0.0625, ((0, 4), (1, 8))),
        "queries": draw_queries(jax.random.fold_in(key_list[10], 71), 0),
        "key_cache": draw_key_cache(jax.random.fold_in(key_list[10], 71), 0),
        "value_cache": scatter_about(key_list[8], (ROWS, CTX, HD), 1.0, 6.0, ((0, 32),)),
        "lengths": draw_lengths(jax.random.fold_in(key_list[10], 71), 0),
    }


def layer_norm(tokens, gain):
    values = tokens.astype(jnp.float32)
    centred = values - lax.optimization_barrier(jnp.mean(values, axis=-1, keepdims=True))
    spread = lax.optimization_barrier(jnp.mean(centred * centred, axis=-1, keepdims=True))
    return (centred * lax.rsqrt(spread + 1e-05) * gain).astype(jnp.bfloat16)

def attend_row(inputs):
    query, keys, values, length, key_new, value_new = inputs
    grouped = query.reshape(HEADS, HD).astype(jnp.float32)
    scale = 1.0 / HD ** 0.5
    scores = jnp.dot(grouped, keys.astype(jnp.float32).T, preferred_element_type=jnp.float32) * scale
    own = jnp.dot(grouped, key_new.astype(jnp.float32), preferred_element_type=jnp.float32) * scale
    live = jnp.arange(CTX) < length
    scores = jnp.where(live[None, :], scores, -jnp.inf)
    top = jnp.maximum(lax.optimization_barrier(jnp.max(scores, axis=-1)), own)
    weights = jnp.exp(scores - top[:, None])
    own_weight = jnp.exp(own - top)
    total = lax.optimization_barrier(jnp.sum(weights, axis=-1)) + own_weight
    probs = (weights / total[:, None]).astype(jnp.bfloat16)
    own_prob = (own_weight / total).astype(jnp.bfloat16)
    context = jnp.dot(probs, values, preferred_element_type=jnp.float32)
    context = context + own_prob.astype(jnp.float32)[:, None] * value_new.astype(jnp.float32)[None, :]
    return context.reshape(-1).astype(jnp.bfloat16)

def reference(tokens, gain, w_gate, w_up, w_down, w_kv, queries, key_cache, value_cache, lengths):
    normed = layer_norm(tokens, gain)
    gate = jnp.dot(normed, w_gate, preferred_element_type=jnp.float32)
    up = jnp.dot(normed, w_up, preferred_element_type=jnp.float32)
    hidden = (jax.nn.silu(gate) * up).astype(jnp.bfloat16)
    ffn = jnp.dot(hidden, w_down, preferred_element_type=jnp.float32)
    mixed = (tokens.astype(jnp.float32) + ffn).astype(jnp.bfloat16)
    fresh = jnp.dot(normed, w_kv.reshape(D, 2 * HD), preferred_element_type=jnp.float32)
    key_new = fresh[:, :HD].astype(jnp.bfloat16)
    value_new = fresh[:, HD:].astype(jnp.bfloat16)
    context = lax.map(attend_row, (queries, key_cache, value_cache, lengths, key_new, value_new))
    return (mixed, context)
```

```python
import functools
import math

import jax
import jax.numpy as jnp
from jax import lax
from jax.experimental import pallas as pl
from jax.experimental.pallas import tpu as pltpu
from jax.sharding import PartitionSpec as P

HD = 256
F32 = jnp.float32
BF16 = jnp.bfloat16
VMEM_LIMIT = 40 * 1024 * 1024


def params():
    return pltpu.CompilerParams(vmem_limit_bytes=VMEM_LIMIT)


def tile_of(width, most):
    return max(t for t in range(128, most + 1, 128) if width % t == 0)


def swap(x, axis, size, bits):
    return lax.ppermute(x, axis, [(i, i ^ bits) for i in range(size)])


def layer_norm(tokens, gain):
    values = tokens.astype(F32)
    centred = values - jnp.mean(values, axis=-1, keepdims=True)
    spread = jnp.mean(centred * centred, axis=-1, keepdims=True)
    return (centred * lax.rsqrt(spread + 1e-05) * gain).astype(BF16)


def assemble_kernel(dest_ref, *refs):
    pieces, out_ref = refs[:-1], refs[-1]
    for q, piece in enumerate(pieces):
        out_ref[dest_ref[q]] = piece[...]


def assemble(dest, pieces):
    count = len(pieces)
    rows, width = pieces[0].shape
    size = count * rows * width
    return pl.pallas_call(
        assemble_kernel,
        grid_spec=pltpu.PrefetchScalarGridSpec(
            num_scalar_prefetch=1,
            grid=(1,),
            in_specs=[pl.BlockSpec((rows, width), lambda i, d: (0, 0))] * count,
            out_specs=pl.BlockSpec((count, rows, width), lambda i, d: (0, 0, 0)),
        ),
        out_shape=jax.ShapeDtypeStruct((count, rows, width), pieces[0].dtype),
        compiler_params=params(),
        cost_estimate=pl.CostEstimate(flops=size, bytes_accessed=4 * size, transcendentals=0),
    )(dest, *pieces)


def gate_up_kernel(x_ref, gate_ref, up_ref, keep_ref, send_ref):
    half = keep_ref.shape[1]
    x = x_ref[...]
    for at, weight in enumerate((gate_ref, up_ref)):
        value = jnp.dot(x, weight[...], preferred_element_type=F32)
        keep_ref[at] = value[:half]
        send_ref[at] = value[half:].astype(BF16)


def gate_up(x, w_gate, w_up, start, width):
    rows, depth = x.shape
    half = rows // 2
    tile = tile_of(width, 384)
    first = start // tile
    weight = pl.BlockSpec((depth, tile), lambda j: (0, first + j))
    part = pl.BlockSpec((2, half, tile), lambda j: (0, 0, j))
    return pl.pallas_call(
        gate_up_kernel,
        grid=(width // tile,),
        in_specs=[pl.BlockSpec((rows, depth), lambda j: (0, 0)), weight, weight],
        out_specs=[part, part],
        out_shape=[
            jax.ShapeDtypeStruct((2, half, width), F32),
            jax.ShapeDtypeStruct((2, half, width), BF16),
        ],
        compiler_params=params(),
        cost_estimate=pl.CostEstimate(
            flops=4 * rows * depth * width,
            bytes_accessed=4 * depth * width + 2 * rows * depth + 6 * rows * width,
            transcendentals=0,
        ),
    )(x, w_gate, w_up)


def down_kernel(has_sum, last, dest_ref, *refs):
    hidden, refs = refs[:4], refs[4:]
    weight_ref, refs = refs[0], refs[1:]
    x = jnp.concatenate([h[...] for h in hidden], axis=0)
    value = jnp.dot(x, weight_ref[...], preferred_element_type=F32)
    if has_sum:
        value = value + refs[0][...]
        refs = refs[1:]
    if not last:
        refs[0][...] = value
        return
    keep_ref, send_ref, scratch = refs
    groups = scratch.shape[0]
    scratch[...] = value.reshape(scratch.shape)
    for q in range(0, groups, 2):
        keep_ref[q // 2] = scratch[dest_ref[q]]
        send_ref[q // 2] = scratch[dest_ref[q + 1]].astype(BF16)


def down(dest, hidden, w_down, start, total, groups, last):
    part_rows, depth = hidden[0].shape
    rows = 4 * part_rows
    width = w_down.shape[1]
    tile = tile_of(width, 384)
    first = start // depth
    in_specs = [pl.BlockSpec((part_rows, depth), lambda j, d: (0, 0))] * 4
    in_specs.append(pl.BlockSpec((depth, tile), lambda j, d: (first, j)))
    args = [*hidden, w_down]
    block = pl.BlockSpec((rows, tile), lambda j, d: (0, j))
    if total is not None:
        in_specs.append(block)
        args.append(total)
    aliases = {}
    scratch = []
    if last:
        shape = (groups // 2, rows // groups, width)
        part = pl.BlockSpec((groups // 2, rows // groups, tile), lambda j, d: (0, 0, j))
        out_specs = [part, part]
        out_shape = [jax.ShapeDtypeStruct(shape, F32), jax.ShapeDtypeStruct(shape, BF16)]
        scratch = [pltpu.VMEM((groups, rows // groups, tile), F32)]
    else:
        out_specs = block
        out_shape = jax.ShapeDtypeStruct((rows, width), F32)
    return pl.pallas_call(
        functools.partial(down_kernel, total is not None, last),
        grid_spec=pltpu.PrefetchScalarGridSpec(
            num_scalar_prefetch=1,
            grid=(width // tile,),
            in_specs=in_specs,
            out_specs=out_specs,
            scratch_shapes=scratch,
        ),
        out_shape=out_shape,
        input_output_aliases=aliases,
        compiler_params=params(),
        cost_estimate=pl.CostEstimate(
            flops=2 * rows * depth * width,
            bytes_accessed=2 * depth * width + 8 * rows * width,
            transcendentals=0,
        ),
    )(dest, *args)


def cache_kernel(scale, lengths_ref, query_ref, key_ref, value_ref, acc_ref, top_ref, sum_ref):
    length = lengths_ref[pl.program_id(0)]
    scores = scale * lax.dot_general(
        query_ref[0], key_ref[0], (((1,), (1,)), ((), ())), preferred_element_type=F32
    )
    heads = scores.shape[0]
    live = lax.broadcasted_iota(jnp.int32, scores.shape, 1) < length
    scores = jnp.where(live, scores, -jnp.inf)
    top = jnp.max(scores, axis=1, keepdims=True)
    weights = jnp.exp(scores - top)
    high = weights.astype(BF16)
    low = (weights - high.astype(F32)).astype(BF16)
    both = jnp.dot(
        jnp.concatenate((high, low), axis=0), value_ref[0], preferred_element_type=F32
    )
    acc_ref[0] = both[:heads] + both[heads:]
    top_ref[0] = top
    sum_ref[0] = jnp.sum(weights, axis=1, keepdims=True)


def attend_cache(grouped, key_cache, value_cache, lengths):
    batch, heads, depth = grouped.shape
    span = key_cache.shape[1]
    row = lambda r, n: (r, 0, 0)
    cache = pl.BlockSpec((1, span, depth), row)
    return pl.pallas_call(
        functools.partial(cache_kernel, 1.0 / math.sqrt(depth)),
        grid_spec=pltpu.PrefetchScalarGridSpec(
            num_scalar_prefetch=1,
            grid=(batch,),
            in_specs=[pl.BlockSpec((1, heads, depth), row), cache, cache],
            out_specs=[
                pl.BlockSpec((1, heads, depth), row),
                pl.BlockSpec((1, heads, 1), row),
                pl.BlockSpec((1, heads, 1), row),
            ],
        ),
        out_shape=[
            jax.ShapeDtypeStruct((batch, heads, depth), F32),
            jax.ShapeDtypeStruct((batch, heads, 1), F32),
            jax.ShapeDtypeStruct((batch, heads, 1), F32),
        ],
        compiler_params=params(),
        cost_estimate=pl.CostEstimate(
            flops=6 * batch * heads * span * depth,
            bytes_accessed=4 * batch * span * depth,
            transcendentals=batch * heads * span,
        ),
    )(lengths, grouped, key_cache, value_cache)


def attend_new(grouped, cached, key_new, value_new):
    acc, top_cached, sum_cached = cached
    batch = grouped.shape[0]
    scale = 1.0 / math.sqrt(grouped.shape[2])
    own = jnp.einsum("rhd,rd->rh", grouped, key_new, preferred_element_type=F32)
    own = own[:, :, None] * scale
    top = jnp.maximum(top_cached, own)
    old = jnp.exp(top_cached - top)
    new = jnp.exp(own - top)
    total = sum_cached * old + new
    context = (acc * old + new * value_new.astype(F32)[:, None, :]) / total
    return context.astype(BF16).reshape(batch, -1)


def body(n_gx, n_gy, tokens, gain, w_gate, w_up, w_down, w_kv, queries, key_cache, value_cache, lengths):
    gx = lax.axis_index("gx")
    gy = lax.axis_index("gy")
    swap_x = lambda x, bits: swap(x, "gx", n_gx, bits)
    swap_y = lambda x, bits: swap(x, "gy", n_gy, bits)
    blocks = n_gx // n_gy

    group = gx ^ jnp.arange(n_gx, dtype=jnp.int32)
    turn = (group // blocks) ^ gy
    dest = (((turn & 1) << 1) | (turn >> 1)) * blocks + group % blocks

    normed = layer_norm(tokens, gain)
    grid_in = lax.all_to_all(normed, "gy", split_axis=1, concat_axis=0, tiled=True)
    group_rows = grid_in.shape[0]
    pieces = [None] * n_gx
    for q in range(0, n_gx, 2):
        pieces[q] = swap_x(grid_in, q) if q else grid_in
    for q in range(0, n_gx, 2):
        pieces[q + 1] = swap_x(pieces[q], 1)
    x = assemble(dest, pieces).reshape(n_gx * group_rows, -1)
    rows = x.shape[0]

    batch = tokens.shape[0]
    grouped = queries.reshape(batch, -1, HD)
    cached = attend_cache(grouped, key_cache, value_cache, lengths)

    slab = w_kv.shape[1]
    part = jnp.dot(
        lax.dynamic_slice_in_dim(x, gx * slab, slab, 1), w_kv[0], preferred_element_type=F32
    )
    order = jnp.arange(n_gx, dtype=jnp.int32)
    turn_abs = (order // blocks) ^ gy
    place = (((turn_abs & 1) << 1) | (turn_abs >> 1)) * blocks + order % blocks
    part = part.reshape(n_gx, group_rows, -1)[place].reshape(rows, -1)
    fresh = lax.psum_scatter(part, ("gx", "gy"), scatter_dimension=0, tiled=True)
    key_new = fresh[:, :HD].astype(BF16)
    value_new = fresh[:, HD:].astype(BF16)

    hidden_cols = w_gate.shape[1]
    chunks = max(c for c in (1, 2, 3, 4) if hidden_cols % (128 * c) == 0)
    width = hidden_cols // chunks
    quarter = rows // 4
    total = None
    for c in range(chunks):
        keep, send = gate_up(x, w_gate, w_up, c * width, width)
        near = keep + swap_y(send, 1).astype(F32)
        pair = near[:, :quarter] + swap_y(near[:, quarter:].astype(BF16), 2).astype(F32)
        own = (jax.nn.silu(pair[0]) * pair[1]).astype(BF16)
        across = swap_y(own, 2)
        hidden = (own, across, swap_y(own, 1), swap_y(across, 1))
        total = down(dest, hidden, w_down, c * width, total, n_gx, c == chunks - 1)

    keep, send = total
    near = keep + swap_x(send, 1).astype(F32)
    back = near[0]
    for t in range(1, n_gx // 2):
        back = back + swap_x(near[t].astype(BF16), 2 * t).astype(F32)
    ffn = lax.all_to_all(back, "gy", split_axis=0, concat_axis=1, tiled=True)
    mixed = (tokens.astype(F32) + ffn).astype(BF16)
    context = attend_new(grouped, cached, key_new, value_new)
    return (mixed, context)


def solution(mesh):
    sizes = dict(mesh.shape)
    return jax.shard_map(
        functools.partial(body, sizes["gx"], sizes["gy"]),
        mesh=mesh,
        in_specs=(
            P(("gx", "gy"), None),
            P(),
            P("gy", "gx"),
            P("gy", "gx"),
            P("gx", "gy"),
            P("gy", "gx", None),
            P(("gx", "gy"), None),
            P(("gx", "gy"), None, None),
            P(("gx", "gy"), None, None),
            P(("gx", "gy")),
        ),
        out_specs=(P(("gx", "gy"), None), P(("gx", "gy"), None)),
        check_vma=False,
    )
```

```python
import functools
import math

import jax
import jax.numpy as jnp
from jax import lax
from jax.experimental import pallas as pl
from jax.experimental.pallas import tpu as pltpu
from jax.sharding import PartitionSpec as P

HD = 256
F32 = jnp.float32
BF16 = jnp.bfloat16
MIB = 1024 * 1024
WHOLE = pl.BlockSpec(memory_space=pltpu.VMEM)
SCALARS = pl.BlockSpec(memory_space=pltpu.SMEM)
ANYWHERE = pl.BlockSpec(memory_space=pl.ANY)
ORDER = (0, 2, 1, 3)


def params(mib):
    return pltpu.CompilerParams(vmem_limit_bytes=mib * MIB)


def cost(flops, moved, transcendentals=0):
    return pl.CostEstimate(flops=flops, bytes_accessed=moved, transcendentals=transcendentals)


def tile_of(width, most):
    return max(t for t in range(128, most + 1, 128) if width % t == 0)


def swap(x, axis, size, bits):
    return lax.ppermute(x, axis, [(i, i ^ bits) for i in range(size)])


def norm_kernel(tokens_ref, gain_ref, out_ref):
    copies, blocks, _, width = out_ref.shape
    values = tokens_ref[...].astype(F32)
    centred = values - jnp.mean(values, axis=-1, keepdims=True)
    spread = jnp.mean(centred * centred, axis=-1, keepdims=True)
    normed = (centred * lax.rsqrt(spread + 1e-05) * gain_ref[...]).astype(BF16)
    for b in range(blocks):
        part = normed[:, b * width : (b + 1) * width]
        for c in range(copies):
            out_ref[c, b] = part


def norm(tokens, gain, n_gx, n_gy):
    batch, channels = tokens.shape
    return pl.pallas_call(
        norm_kernel,
        in_specs=[WHOLE, WHOLE],
        out_specs=WHOLE,
        out_shape=jax.ShapeDtypeStruct((n_gx, n_gy, batch, channels // n_gy), BF16),
        compiler_params=params(8),
        cost_estimate=cost(10 * tokens.size, 2 * n_gx * tokens.size),
    )(tokens, gain.reshape(1, -1))


def assemble_kernel(gy_ref, rows_ref, out_ref):
    devices, batch, _ = rows_ref.shape
    quarter = devices // 4
    pack = 16 // batch
    for at, turn in enumerate(ORDER):
        base = (gy_ref[0] ^ turn) * quarter
        for i in range(0, quarter, pack):
            tall = jnp.concatenate(
                [rows_ref[base + i + k].astype(F32) for k in range(pack)], axis=0
            )
            start = (at * quarter + i) * batch
            out_ref[start : start + 16] = tall.astype(BF16)


def assemble(gy, rows):
    devices, batch, width = rows.shape
    return pl.pallas_call(
        assemble_kernel,
        in_specs=[SCALARS, WHOLE],
        out_specs=WHOLE,
        out_shape=jax.ShapeDtypeStruct((devices * batch, width), BF16),
        compiler_params=params(12),
        cost_estimate=cost(2 * rows.size, 4 * rows.size),
    )(gy, rows)


def spread_rows(out_ref, value, gy, columns=slice(None)):
    devices, batch, _ = out_ref.shape
    quarter = devices // 4
    for at, turn in enumerate(ORDER):
        base = (gy ^ turn) * quarter
        for i in range(quarter):
            start = (at * quarter + i) * batch
            out_ref[base + i, :, columns] = value[start : start + batch].astype(out_ref.dtype)


def gate_up_tile(x, weights, at, tile, keep_ref, send_ref):
    half = keep_ref.shape[1]
    for k, weight in enumerate(weights):
        value = jnp.dot(x, weight, preferred_element_type=F32)
        keep_ref[k, :, at : at + tile] = value[:half]
        send_ref[k, :, at : at + tile] = value[half:].astype(BF16)


def gate_up_kernel(start, tile, x_ref, gate_ref, up_ref, after_ref, keep_ref, send_ref, slots, sems):
    del after_ref
    width = keep_ref.shape[2]
    depth = x_ref.shape[1]
    copies = []
    for at in range(0, width, tile):
        for k, source in enumerate((gate_ref, up_ref)):
            copies.append(
                pltpu.make_async_copy(
                    source.at[:, pl.ds(start + at, tile)],
                    slots.at[k, at // tile],
                    sems.at[k, at // tile],
                )
            )
    for copy in copies:
        copy.start()
    x = x_ref[...]
    for n in range(width // tile):
        for k in range(2):
            copies[2 * n + k].wait()
        gate_up_tile(x, [slots[k, n] for k in range(2)], n * tile, tile, keep_ref, send_ref)


def gate_up_ready_kernel(tile, x_ref, gate_ref, up_ref, keep_ref, send_ref):
    x = x_ref[...]
    for at in range(0, keep_ref.shape[2], tile):
        weights = [ref[:, at : at + tile] for ref in (gate_ref, up_ref)]
        gate_up_tile(x, weights, at, tile, keep_ref, send_ref)


def gate_up_shapes(rows, width):
    half = rows // 2
    return [
        jax.ShapeDtypeStruct((2, half, width), F32),
        jax.ShapeDtypeStruct((2, half, width), BF16),
    ]


def gate_up_ready(x, gate, up):
    rows, depth = x.shape
    width = gate.shape[1]
    return pl.pallas_call(
        functools.partial(gate_up_ready_kernel, tile_of(width, 384)),
        in_specs=[WHOLE, WHOLE, WHOLE],
        out_specs=[WHOLE, WHOLE],
        out_shape=gate_up_shapes(rows, width),
        compiler_params=params(16),
        cost_estimate=cost(4 * rows * depth * width, 2 * rows * depth),
    )(x, gate, up)


def gate_up(x, w_gate, w_up, start, width, after):
    rows, depth = x.shape
    tile = tile_of(width, 384)
    count = width // tile
    return pl.pallas_call(
        functools.partial(gate_up_kernel, start, tile),
        in_specs=[WHOLE, ANYWHERE, ANYWHERE, ANYWHERE],
        out_specs=[WHOLE, WHOLE],
        out_shape=gate_up_shapes(rows, width),
        scratch_shapes=[
            pltpu.VMEM((2, count, depth, tile), BF16),
            pltpu.SemaphoreType.DMA((2, count)),
        ],
        compiler_params=params(20),
        cost_estimate=cost(4 * rows * depth * width, 4 * depth * width),
    )(x, w_gate, w_up, after)


def down_kernel(start, tile, has_sum, last, gy_ref, *refs):
    hidden, (weight_ref, *refs) = refs[:4], refs[4:]
    sum_ref = refs.pop(0) if has_sum else None
    out_ref, slots, sems = refs
    depth = hidden[0].shape[1]
    width = weight_ref.shape[1]
    copies = [
        pltpu.make_async_copy(
            weight_ref.at[pl.ds(start, depth), pl.ds(at, tile)],
            slots.at[at // tile],
            sems.at[at // tile],
        )
        for at in range(0, width, tile)
    ]
    for copy in copies:
        copy.start()
    x = jnp.concatenate([h[...] for h in hidden], axis=0)
    gy = gy_ref[0]
    for n, copy in enumerate(copies):
        columns = slice(n * tile, (n + 1) * tile)
        copy.wait()
        value = jnp.dot(x, slots[n], preferred_element_type=F32)
        if has_sum:
            value = value + sum_ref[:, columns]
        if last:
            spread_rows(out_ref, value, gy, columns)
        else:
            out_ref[:, columns] = value


def down(gy, hidden, w_down, start, total, devices, last):
    part_rows, depth = hidden[0].shape
    rows = 4 * part_rows
    width = w_down.shape[1]
    tile = tile_of(width, 384)
    count = width // tile
    args = [gy, *hidden, w_down]
    in_specs = [SCALARS] + [WHOLE] * 4 + [ANYWHERE]
    if total is not None:
        args.append(total)
        in_specs.append(WHOLE)
    shape = (devices, rows // devices, width) if last else (rows, width)
    return pl.pallas_call(
        functools.partial(down_kernel, start, tile, total is not None, last),
        in_specs=in_specs,
        out_specs=WHOLE,
        out_shape=jax.ShapeDtypeStruct(shape, BF16 if last else F32),
        scratch_shapes=[
            pltpu.VMEM((count, depth, tile), BF16),
            pltpu.SemaphoreType.DMA((count,)),
        ],
        compiler_params=params(20),
        cost_estimate=cost(2 * rows * depth * width, 2 * depth * width),
    )(*args)


def finish_kernel(tokens_ref, sums_ref, out_ref):
    sources, blocks, _, width = sums_ref.shape
    for b in range(blocks):
        columns = slice(b * width, (b + 1) * width)
        ffn = sums_ref[0, b].astype(F32)
        for s in range(1, sources):
            ffn = ffn + sums_ref[s, b].astype(F32)
        out_ref[:, columns] = (tokens_ref[:, columns].astype(F32) + ffn).astype(BF16)


def finish(tokens, sums):
    return pl.pallas_call(
        finish_kernel,
        in_specs=[WHOLE, WHOLE],
        out_specs=WHOLE,
        out_shape=jax.ShapeDtypeStruct(tokens.shape, BF16),
        compiler_params=params(8),
        cost_estimate=cost(sums.size, 2 * sums.size),
    )(tokens, sums)


def fresh_kernel(gy_ref, x_ref, weight_ref, out_ref):
    value = jnp.dot(x_ref[...], weight_ref[0], preferred_element_type=F32)
    spread_rows(out_ref, value, gy_ref[0])


def fresh_part(gy, x, w_kv, devices):
    rows, depth = x.shape
    columns = w_kv.shape[2]
    return pl.pallas_call(
        fresh_kernel,
        in_specs=[SCALARS, WHOLE, WHOLE],
        out_specs=WHOLE,
        out_shape=jax.ShapeDtypeStruct((devices, rows // devices, columns), F32),
        compiler_params=params(8),
        cost_estimate=cost(2 * rows * depth * columns, 2 * depth * columns),
    )(gy, x, w_kv)


def cache_kernel(
    scale, tile, lengths_ref, query_ref, key_ref, value_ref, gate_ref, up_ref, after_ref,
    acc_ref, top_ref, sum_ref, gate_out, up_out, keys, values, cache_sems, weight_sems,
):
    del after_ref
    batch = query_ref.shape[0]
    caches = [
        [
            pltpu.make_async_copy(source.at[r], slots.at[r], cache_sems.at[k, r])
            for k, (source, slots) in enumerate(((key_ref, keys), (value_ref, values)))
        ]
        for r in range(batch)
    ]
    weights = [
        pltpu.make_async_copy(
            source.at[:, pl.ds(at, tile)],
            target.at[:, pl.ds(at, tile)],
            weight_sems.at[k, at // tile],
        )
        for at in range(0, gate_out.shape[1], tile)
        for k, (source, target) in enumerate(((gate_ref, gate_out), (up_ref, up_out)))
    ]
    for pair in caches:
        for copy in pair:
            copy.start()
    for copy in weights:
        copy.start()
    for r in range(batch):
        caches[r][0].wait()
        scores = scale * lax.dot_general(
            query_ref[r], keys[r], (((1,), (1,)), ((), ())), preferred_element_type=F32
        )
        heads = scores.shape[0]
        live = lax.broadcasted_iota(jnp.int32, scores.shape, 1) < lengths_ref[r]
        scores = jnp.where(live, scores, -jnp.inf)
        top = jnp.max(scores, axis=1, keepdims=True)
        chance = jnp.exp(scores - top)
        high = chance.astype(BF16)
        low = (chance - high.astype(F32)).astype(BF16)
        caches[r][1].wait()
        both = jnp.dot(
            jnp.concatenate((high, low), axis=0), values[r], preferred_element_type=F32
        )
        acc_ref[r] = both[:heads] + both[heads:]
        top_ref[r] = top
        sum_ref[r] = jnp.sum(chance, axis=1, keepdims=True)
    for copy in weights:
        copy.wait()


def attend_cache(grouped, key_cache, value_cache, lengths, w_gate, w_up, width, after):
    batch, heads, depth = grouped.shape
    span = key_cache.shape[1]
    tall = w_gate.shape[0]
    tile = tile_of(width, 384)
    *cached, gate, up = pl.pallas_call(
        functools.partial(cache_kernel, 1.0 / math.sqrt(depth), tile),
        in_specs=[SCALARS, WHOLE] + [ANYWHERE] * 5,
        out_specs=[WHOLE] * 5,
        out_shape=[
            jax.ShapeDtypeStruct((batch, heads, depth), F32),
            jax.ShapeDtypeStruct((batch, heads, 1), F32),
            jax.ShapeDtypeStruct((batch, heads, 1), F32),
            pltpu.VMEM((tall, width), BF16),
            pltpu.VMEM((tall, width), BF16),
        ],
        scratch_shapes=[
            pltpu.VMEM((batch, span, depth), BF16),
            pltpu.VMEM((batch, span, depth), BF16),
            pltpu.SemaphoreType.DMA((2, batch)),
            pltpu.SemaphoreType.DMA((2, width // tile)),
        ],
        compiler_params=params(24),
        cost_estimate=cost(
            6 * batch * heads * span * depth,
            4 * batch * span * depth + 4 * tall * width,
            batch * heads * span,
        ),
    )(lengths, grouped, key_cache, value_cache, w_gate, w_up, after)
    return cached, gate, up


def attend_new(grouped, cached, key_new, value_new):
    acc, top_cached, sum_cached = cached
    batch = grouped.shape[0]
    scale = 1.0 / math.sqrt(grouped.shape[2])
    own = jnp.einsum("rhd,rd->rh", grouped, key_new, preferred_element_type=F32)
    own = own[:, :, None] * scale
    top = jnp.maximum(top_cached, own)
    old = jnp.exp(top_cached - top)
    new = jnp.exp(own - top)
    total = sum_cached * old + new
    context = (acc * old + new * value_new.astype(F32)[:, None, :]) / total
    return context.astype(BF16).reshape(batch, -1)


def chunk_widths(columns):
    units = columns // 128
    first = units // 2
    second = (units - first) // 2
    return [128 * u for u in (first, second, units - first - second)]


def body(n_gx, n_gy, tokens, gain, w_gate, w_up, w_down, w_kv, queries, key_cache, value_cache, lengths):
    gx = lax.axis_index("gx")
    gy = lax.axis_index("gy").astype(jnp.int32).reshape(1)
    swap_gy = lambda x, bits: swap(x, "gy", n_gy, bits)
    exchange = lambda x: lax.all_to_all(x, ("gx", "gy"), split_axis=0, concat_axis=0, tiled=True)
    devices = n_gx * n_gy
    batch = tokens.shape[0]
    widths = chunk_widths(w_gate.shape[1])

    normed = norm(tokens, gain, n_gx, n_gy)
    gathered = exchange(normed.reshape(devices, batch, -1))
    grouped = queries.reshape(batch, -1, HD)
    cached, gate, up = attend_cache(
        grouped, key_cache, value_cache, lengths, w_gate, w_up, widths[0], normed
    )
    x = assemble(gy, gathered)
    rows = x.shape[0]
    quarter = rows // 4

    sums = []
    start = 0
    for c, width in enumerate(widths):
        if c == 0:
            keep, send = gate_up_ready(x, gate, up)
        else:
            keep, send = gate_up(x, w_gate, w_up, start, width, sums[0][2] if c == 1 else send)
        core = swap_gy(send, 1)
        across = (keep[:, quarter:] + core[:, quarter:].astype(F32)).astype(BF16)
        sums.append((keep, core, across))
        start += width

    slab = w_kv.shape[1]
    part = fresh_part(gy, lax.dynamic_slice_in_dim(x, gx * slab, slab, 1), w_kv, devices)
    fresh = jnp.sum(exchange(part), axis=0)
    key_new = fresh[:, :HD].astype(BF16)
    value_new = fresh[:, HD:].astype(BF16)

    start = 0
    total = None
    for c, (keep, core, across) in enumerate(sums):
        pair = keep[:, :quarter] + core[:, :quarter].astype(F32) + swap_gy(across, 2).astype(F32)
        own = (jax.nn.silu(pair[0]) * pair[1]).astype(BF16)
        far = swap_gy(own, 2)
        hidden = (own, far, swap_gy(own, 1), swap_gy(far, 1))
        total = down(gy, hidden, w_down, start, total, devices, c == len(sums) - 1)
        start += widths[c]

    ffn = exchange(total)
    mixed = finish(tokens, ffn.reshape(n_gx, n_gy, batch, -1))
    context = attend_new(grouped, cached, key_new, value_new)
    return (mixed, context)


def solution(mesh):
    sizes = dict(mesh.shape)
    return jax.shard_map(
        functools.partial(body, sizes["gx"], sizes["gy"]),
        mesh=mesh,
        in_specs=(
            P(("gx", "gy"), None),
            P(),
            P("gy", "gx"),
            P("gy", "gx"),
            P("gx", "gy"),
            P("gy", "gx", None),
            P(("gx", "gy"), None),
            P(("gx", "gy"), None, None),
            P(("gx", "gy"), None, None),
            P(("gx", "gy")),
        ),
        out_specs=(P(("gx", "gy"), None), P(("gx", "gy"), None)),
        check_vma=False,
    )
```

```python
import functools
import math

import jax
import jax.numpy as jnp
from jax import lax
from jax.experimental import pallas as pl
from jax.experimental.pallas import tpu as pltpu
from jax.sharding import PartitionSpec as P

HD = 256
F32 = jnp.float32
BF16 = jnp.bfloat16
MIB = 1024 * 1024
WHOLE = pl.BlockSpec(memory_space=pltpu.VMEM)
SCALARS = pl.BlockSpec(memory_space=pltpu.SMEM)
ANYWHERE = pl.BlockSpec(memory_space=pl.ANY)
ORDER = (0, 2, 1, 3)


def params(mib):
    return pltpu.CompilerParams(vmem_limit_bytes=mib * MIB)


def cost(flops, moved, transcendentals=0):
    return pl.CostEstimate(flops=flops, bytes_accessed=moved, transcendentals=transcendentals)


def tile_of(width, most):
    return max(t for t in range(128, most + 1, 128) if width % t == 0)


def in_hbm(x):
    return pltpu.with_memory_space_constraint(x, pltpu.HBM)


def swap(x, axis, size, bits):
    return lax.ppermute(x, axis, [(i, i ^ bits) for i in range(size)])


def norm_kernel(tokens_hbm, gain_hbm, out_ref, tokens_ref, gain_ref, sems):
    copies, blocks, _, width = out_ref.shape
    moves = [
        pltpu.make_async_copy(source, target, sems.at[k])
        for k, (source, target) in enumerate(((tokens_hbm, tokens_ref), (gain_hbm, gain_ref)))
    ]
    for move in moves:
        move.start()
    for move in moves:
        move.wait()
    values = tokens_ref[...].astype(F32)
    centred = values - jnp.mean(values, axis=-1, keepdims=True)
    spread = jnp.mean(centred * centred, axis=-1, keepdims=True)
    normed = (centred * lax.rsqrt(spread + 1e-05) * gain_ref[...]).astype(BF16)
    for b in range(blocks):
        part = normed[:, b * width : (b + 1) * width]
        for c in range(copies):
            out_ref[c, b] = part


def norm(tokens, gain, n_gx, n_gy):
    batch, channels = tokens.shape
    return pl.pallas_call(
        norm_kernel,
        in_specs=[ANYWHERE, ANYWHERE],
        out_specs=WHOLE,
        out_shape=jax.ShapeDtypeStruct((n_gx, n_gy, batch, channels // n_gy), BF16),
        scratch_shapes=[
            pltpu.VMEM((batch, channels), BF16),
            pltpu.VMEM((1, channels), F32),
            pltpu.SemaphoreType.DMA((2,)),
        ],
        compiler_params=params(8),
        cost_estimate=cost(10 * tokens.size, 2 * n_gx * tokens.size),
    )(in_hbm(tokens), in_hbm(gain.reshape(1, -1)))


def assemble_kernel(gy_ref, rows_ref, out_ref):
    devices, batch, _ = rows_ref.shape
    quarter = devices // 4
    pack = 16 // batch
    for at, turn in enumerate(ORDER):
        base = (gy_ref[0] ^ turn) * quarter
        for i in range(0, quarter, pack):
            tall = jnp.concatenate(
                [rows_ref[base + i + k].astype(F32) for k in range(pack)], axis=0
            )
            start = (at * quarter + i) * batch
            out_ref[start : start + 16] = tall.astype(BF16)


def assemble(gy, rows):
    devices, batch, width = rows.shape
    return pl.pallas_call(
        assemble_kernel,
        in_specs=[SCALARS, WHOLE],
        out_specs=WHOLE,
        out_shape=jax.ShapeDtypeStruct((devices * batch, width), BF16),
        compiler_params=params(4),
        cost_estimate=cost(2 * rows.size, 4 * rows.size),
    )(gy, rows)


def spread_rows(out_ref, value, gy, columns=slice(None)):
    devices, batch, _ = out_ref.shape
    quarter = devices // 4
    for at, turn in enumerate(ORDER):
        base = (gy ^ turn) * quarter
        for i in range(quarter):
            start = (at * quarter + i) * batch
            out_ref[base + i, :, columns] = value[start : start + batch].astype(out_ref.dtype)


def gate_up_tile(x, weights, at, tile, keep_ref, send_ref):
    half = keep_ref.shape[1]
    for k, weight in enumerate(weights):
        value = jnp.dot(x, weight, preferred_element_type=F32)
        keep_ref[k, :, at : at + tile] = value[:half]
        send_ref[k, :, at : at + tile] = value[half:].astype(BF16)


def gate_up_kernel(start, tile, x_ref, gate_ref, up_ref, after_ref, keep_ref, send_ref, slots, sems):
    del after_ref
    width = keep_ref.shape[2]
    depth = x_ref.shape[1]
    copies = []
    for at in range(0, width, tile):
        for k, source in enumerate((gate_ref, up_ref)):
            copies.append(
                pltpu.make_async_copy(
                    source.at[:, pl.ds(start + at, tile)],
                    slots.at[k, at // tile],
                    sems.at[k, at // tile],
                )
            )
    for copy in copies:
        copy.start()
    x = x_ref[...]
    for n in range(width // tile):
        for k in range(2):
            copies[2 * n + k].wait()
        gate_up_tile(x, [slots[k, n] for k in range(2)], n * tile, tile, keep_ref, send_ref)


def gate_up_ready_kernel(tile, x_ref, gate_ref, up_ref, keep_ref, send_ref):
    x = x_ref[...]
    for at in range(0, keep_ref.shape[2], tile):
        weights = [ref[:, at : at + tile] for ref in (gate_ref, up_ref)]
        gate_up_tile(x, weights, at, tile, keep_ref, send_ref)


def gate_up_shapes(rows, width):
    half = rows // 2
    return [
        jax.ShapeDtypeStruct((2, half, width), F32),
        jax.ShapeDtypeStruct((2, half, width), BF16),
    ]


def gate_up_ready(x, gate, up):
    rows, depth = x.shape
    width = gate.shape[1]
    return pl.pallas_call(
        functools.partial(gate_up_ready_kernel, tile_of(width, 256)),
        in_specs=[WHOLE, WHOLE, WHOLE],
        out_specs=[WHOLE, WHOLE],
        out_shape=gate_up_shapes(rows, width),
        compiler_params=params(8),
        cost_estimate=cost(4 * rows * depth * width, 2 * rows * depth),
    )(x, gate, up)


def gate_up(x, w_gate, w_up, start, width, after):
    rows, depth = x.shape
    tile = tile_of(width, 256)
    count = width // tile
    return pl.pallas_call(
        functools.partial(gate_up_kernel, start, tile),
        in_specs=[WHOLE, ANYWHERE, ANYWHERE, ANYWHERE],
        out_specs=[WHOLE, WHOLE],
        out_shape=gate_up_shapes(rows, width),
        scratch_shapes=[
            pltpu.VMEM((2, count, depth, tile), BF16),
            pltpu.SemaphoreType.DMA((2, count)),
        ],
        compiler_params=params(14),
        cost_estimate=cost(4 * rows * depth * width, 4 * depth * width),
    )(x, in_hbm(w_gate), in_hbm(w_up), after)


def down_kernel(start, tile, has_sum, last, gy_ref, *refs):
    hidden, (weight_ref, *refs) = refs[:4], refs[4:]
    sum_ref = refs.pop(0) if has_sum else None
    out_ref, slots, sems = refs
    depth = hidden[0].shape[1]
    width = weight_ref.shape[1]
    copies = [
        pltpu.make_async_copy(
            weight_ref.at[pl.ds(start, depth), pl.ds(at, tile)],
            slots.at[at // tile],
            sems.at[at // tile],
        )
        for at in range(0, width, tile)
    ]
    for copy in copies:
        copy.start()
    x = jnp.concatenate([h[...] for h in hidden], axis=0)
    gy = gy_ref[0]
    for n, copy in enumerate(copies):
        columns = slice(n * tile, (n + 1) * tile)
        copy.wait()
        value = jnp.dot(x, slots[n], preferred_element_type=F32)
        if has_sum:
            value = value + sum_ref[:, columns]
        if last:
            spread_rows(out_ref, value, gy, columns)
        else:
            out_ref[:, columns] = value


def down(gy, hidden, w_down, start, total, devices, last):
    part_rows, depth = hidden[0].shape
    rows = 4 * part_rows
    width = w_down.shape[1]
    tile = tile_of(width, 256)
    count = width // tile
    args = [gy, *hidden, in_hbm(w_down)]
    in_specs = [SCALARS] + [WHOLE] * 4 + [ANYWHERE]
    if total is not None:
        args.append(total)
        in_specs.append(WHOLE)
    shape = (devices, rows // devices, width) if last else (rows, width)
    return pl.pallas_call(
        functools.partial(down_kernel, start, tile, total is not None, last),
        in_specs=in_specs,
        out_specs=WHOLE,
        out_shape=jax.ShapeDtypeStruct(shape, BF16 if last else F32),
        scratch_shapes=[
            pltpu.VMEM((count, depth, tile), BF16),
            pltpu.SemaphoreType.DMA((count,)),
        ],
        compiler_params=params(14),
        cost_estimate=cost(2 * rows * depth * width, 2 * depth * width),
    )(*args)


def finish_kernel(tokens_ref, sums_ref, out_ref):
    sources, blocks, _, width = sums_ref.shape
    for b in range(blocks):
        columns = slice(b * width, (b + 1) * width)
        ffn = sums_ref[0, b].astype(F32)
        for s in range(1, sources):
            ffn = ffn + sums_ref[s, b].astype(F32)
        out_ref[:, columns] = (tokens_ref[:, columns].astype(F32) + ffn).astype(BF16)


def finish(tokens, sums):
    return pl.pallas_call(
        finish_kernel,
        in_specs=[WHOLE, WHOLE],
        out_specs=WHOLE,
        out_shape=jax.ShapeDtypeStruct(tokens.shape, BF16),
        compiler_params=params(8),
        cost_estimate=cost(sums.size, 2 * sums.size),
    )(tokens, sums)


def fresh_kernel(gy_ref, x_ref, weight_ref, out_ref):
    value = jnp.dot(x_ref[...], weight_ref[0], preferred_element_type=F32)
    spread_rows(out_ref, value, gy_ref[0])


def fresh_part(gy, x, w_kv, devices):
    rows, depth = x.shape
    columns = w_kv.shape[2]
    return pl.pallas_call(
        fresh_kernel,
        in_specs=[SCALARS, WHOLE, WHOLE],
        out_specs=WHOLE,
        out_shape=jax.ShapeDtypeStruct((devices, rows // devices, columns), F32),
        compiler_params=params(8),
        cost_estimate=cost(2 * rows * depth * columns, 2 * depth * columns),
    )(gy, x, w_kv)


def own_first_kernel(gx_ref, gy_ref, sums_ref, after_ref, near_ref, far_ref):
    del after_ref
    for at, turn in enumerate(ORDER):
        device = gx_ref[0] * len(ORDER) + (gy_ref[0] ^ turn)
        (near_ref, far_ref)[at // 2][at % 2] = sums_ref[device]


def own_first(gx, gy, sums, after):
    shape = jax.ShapeDtypeStruct((2, *sums.shape[1:]), sums.dtype)
    return pl.pallas_call(
        own_first_kernel,
        in_specs=[SCALARS, SCALARS, WHOLE, ANYWHERE],
        out_specs=[WHOLE, WHOLE],
        out_shape=[shape, shape],
        compiler_params=params(4),
        cost_estimate=cost(sums.size, 8 * sums.size),
    )(gx, gy, sums, after)


def cache_kernel(
    scale, tile, lengths_ref, query_ref, key_ref, value_ref, gate_ref, up_ref, after_ref,
    acc_ref, top_ref, sum_ref, gate_out, up_out, keys, values, cache_sems, weight_sems,
):
    del after_ref
    batch = query_ref.shape[0]
    caches = [
        [
            pltpu.make_async_copy(source.at[r], slots.at[r], cache_sems.at[k, r])
            for k, (source, slots) in enumerate(((key_ref, keys), (value_ref, values)))
        ]
        for r in range(batch)
    ]
    weights = [
        pltpu.make_async_copy(
            source.at[:, pl.ds(at, tile)],
            target.at[:, pl.ds(at, tile)],
            weight_sems.at[k, at // tile],
        )
        for at in range(0, gate_out.shape[1], tile)
        for k, (source, target) in enumerate(((gate_ref, gate_out), (up_ref, up_out)))
    ]
    for pair in caches:
        for copy in pair:
            copy.start()
    for copy in weights:
        copy.start()
    for r in range(batch):
        caches[r][0].wait()
        scores = scale * lax.dot_general(
            query_ref[r], keys[r], (((1,), (1,)), ((), ())), preferred_element_type=F32
        )
        heads = scores.shape[0]
        live = lax.broadcasted_iota(jnp.int32, scores.shape, 1) < lengths_ref[r]
        scores = jnp.where(live, scores, -jnp.inf)
        top = jnp.max(scores, axis=1, keepdims=True)
        chance = jnp.exp(scores - top)
        high = chance.astype(BF16)
        low = (chance - high.astype(F32)).astype(BF16)
        caches[r][1].wait()
        both = jnp.dot(
            jnp.concatenate((high, low), axis=0), values[r], preferred_element_type=F32
        )
        acc_ref[r] = both[:heads] + both[heads:]
        top_ref[r] = top
        sum_ref[r] = jnp.sum(chance, axis=1, keepdims=True)
    for copy in weights:
        copy.wait()


def attend_cache(grouped, key_cache, value_cache, lengths, w_gate, w_up, width, after):
    batch, heads, depth = grouped.shape
    span = key_cache.shape[1]
    tall = w_gate.shape[0]
    tile = tile_of(width, 256)
    *cached, gate, up = pl.pallas_call(
        functools.partial(cache_kernel, 1.0 / math.sqrt(depth), tile),
        in_specs=[SCALARS, WHOLE] + [ANYWHERE] * 5,
        out_specs=[WHOLE] * 5,
        out_shape=[
            jax.ShapeDtypeStruct((batch, heads, depth), F32),
            jax.ShapeDtypeStruct((batch, heads, 1), F32),
            jax.ShapeDtypeStruct((batch, heads, 1), F32),
            pltpu.VMEM((tall, width), BF16),
            pltpu.VMEM((tall, width), BF16),
        ],
        scratch_shapes=[
            pltpu.VMEM((batch, span, depth), BF16),
            pltpu.VMEM((batch, span, depth), BF16),
            pltpu.SemaphoreType.DMA((2, batch)),
            pltpu.SemaphoreType.DMA((2, width // tile)),
        ],
        compiler_params=params(14),
        cost_estimate=cost(
            6 * batch * heads * span * depth,
            4 * batch * span * depth + 4 * tall * width,
            batch * heads * span,
        ),
    )(lengths, grouped, in_hbm(key_cache), in_hbm(value_cache), in_hbm(w_gate), in_hbm(w_up), after)
    return cached, gate, up


def attend_new(grouped, cached, key_new, value_new):
    acc, top_cached, sum_cached = cached
    batch = grouped.shape[0]
    scale = 1.0 / math.sqrt(grouped.shape[2])
    own = jnp.einsum("rhd,rd->rh", grouped, key_new, preferred_element_type=F32)
    own = own[:, :, None] * scale
    top = jnp.maximum(top_cached, own)
    old = jnp.exp(top_cached - top)
    new = jnp.exp(own - top)
    total = sum_cached * old + new
    context = (acc * old + new * value_new.astype(F32)[:, None, :]) / total
    return context.astype(BF16).reshape(batch, -1)


def chunk_widths(columns):
    unit = 256 if columns % 256 == 0 else 128
    units = columns // unit
    first = units // 2
    second = (units - first) // 2
    return [unit * u for u in (first, second, units - first - second)]


def body(n_gx, n_gy, tokens, gain, w_gate, w_up, w_down, w_kv, queries, key_cache, value_cache, lengths):
    gx = lax.axis_index("gx")
    gy = lax.axis_index("gy").astype(jnp.int32).reshape(1)
    swap_gy = lambda x, bits: swap(x, "gy", n_gy, bits)
    exchange = lambda x: lax.all_to_all(x, ("gx", "gy"), split_axis=0, concat_axis=0, tiled=True)
    devices = n_gx * n_gy
    batch = tokens.shape[0]
    widths = chunk_widths(w_gate.shape[1])

    normed = norm(tokens, gain, n_gx, n_gy)
    gathered = exchange(normed.reshape(devices, batch, -1))
    grouped = queries.reshape(batch, -1, HD)
    cached, gate, up = attend_cache(
        grouped, key_cache, value_cache, lengths, w_gate, w_up, widths[0], normed
    )
    x = assemble(gy, gathered)
    rows = x.shape[0]
    quarter = rows // 4

    sums = []
    start = 0
    for c, width in enumerate(widths):
        if c == 0:
            keep, send = gate_up_ready(x, gate, up)
        else:
            keep, send = gate_up(x, w_gate, w_up, start, width, sums[0][2] if c == 1 else send)
        core = swap_gy(send, 1)
        across = (keep[:, quarter:] + core[:, quarter:].astype(F32)).astype(BF16)
        sums.append((keep, core, across))
        start += width

    slab = w_kv.shape[1]
    part = fresh_part(gy, lax.dynamic_slice_in_dim(x, gx * slab, slab, 1), w_kv, devices)
    over_gx = lax.psum(part, "gx")

    start = 0
    total = None
    for c, (keep, core, across) in enumerate(sums):
        pair = keep[:, :quarter] + core[:, :quarter].astype(F32) + swap_gy(across, 2).astype(F32)
        own = (jax.nn.silu(pair[0]) * pair[1]).astype(BF16)
        far = swap_gy(own, 2)
        hidden = (own, far, swap_gy(own, 1), swap_gy(far, 1))
        total = down(gy, hidden, w_down, start, total, devices, c == len(sums) - 1)
        start += widths[c]
        if c == 0:
            near, far = own_first(gx.astype(jnp.int32).reshape(1), gy, over_gx, total)
            near = near + swap_gy(far, 1)
            fresh = near[0] + swap_gy(near[1], 2)
            key_new = fresh[:, :HD].astype(BF16)
            value_new = fresh[:, HD:].astype(BF16)

    ffn = exchange(total)
    mixed = finish(tokens, ffn.reshape(n_gx, n_gy, batch, -1))
    context = attend_new(grouped, cached, key_new, value_new)
    return (mixed, context)


def solution(mesh):
    sizes = dict(mesh.shape)
    return jax.shard_map(
        functools.partial(body, sizes["gx"], sizes["gy"]),
        mesh=mesh,
        in_specs=(
            P(("gx", "gy"), None),
            P(),
            P("gy", "gx"),
            P("gy", "gx"),
            P("gx", "gy"),
            P("gy", "gx", None),
            P(("gx", "gy"), None),
            P(("gx", "gy"), None, None),
            P(("gx", "gy"), None, None),
            P(("gx", "gy")),
        ),
        out_specs=(P(("gx", "gy"), None), P(("gx", "gy"), None)),
        check_vma=False,
    )
```

```python
import functools
import math

import jax
import jax.numpy as jnp
from jax import lax
from jax.experimental import pallas as pl
from jax.experimental.pallas import tpu as pltpu
from jax.sharding import PartitionSpec as P

HD = 256
F32 = jnp.float32
BF16 = jnp.bfloat16
MIB = 1024 * 1024
WHOLE = pl.BlockSpec(memory_space=pltpu.VMEM)
SCALARS = pl.BlockSpec(memory_space=pltpu.SMEM)
ANYWHERE = pl.BlockSpec(memory_space=pl.ANY)
ORDER = (0, 2, 1, 3)


def params(mib):
    return pltpu.CompilerParams(vmem_limit_bytes=mib * MIB)


def cost(flops, moved, transcendentals=0):
    return pl.CostEstimate(flops=flops, bytes_accessed=moved, transcendentals=transcendentals)


def tile_of(width, most):
    return max(t for t in range(128, most + 1, 128) if width % t == 0)


def in_hbm(x):
    return pltpu.with_memory_space_constraint(x, pltpu.HBM)


def vmem_out(shape, dtype):
    return pltpu.VMEM(shape, dtype)


def in_vmem(x):
    return pltpu.with_memory_space_constraint(x, pltpu.VMEM)


def swap(x, axis, size, bits):
    return lax.ppermute(x, axis, [(i, i ^ bits) for i in range(size)])


def norm_kernel(tokens_hbm, gain_hbm, out_ref, tokens_ref, gain_ref, sems):
    copies, blocks, _, width = out_ref.shape
    moves = [
        pltpu.make_async_copy(source, target, sems.at[k])
        for k, (source, target) in enumerate(((tokens_hbm, tokens_ref), (gain_hbm, gain_ref)))
    ]
    for move in moves:
        move.start()
    for move in moves:
        move.wait()
    values = tokens_ref[...].astype(F32)
    centred = values - jnp.mean(values, axis=-1, keepdims=True)
    spread = jnp.mean(centred * centred, axis=-1, keepdims=True)
    normed = (centred * lax.rsqrt(spread + 1e-05) * gain_ref[...]).astype(BF16)
    for b in range(blocks):
        part = normed[:, b * width : (b + 1) * width]
        for c in range(copies):
            out_ref[c, b] = part


def norm(tokens, gain, n_gx, n_gy):
    batch, channels = tokens.shape
    return pl.pallas_call(
        norm_kernel,
        in_specs=[ANYWHERE, ANYWHERE],
        out_specs=WHOLE,
        out_shape=vmem_out((n_gx, n_gy, batch, channels // n_gy), BF16),
        scratch_shapes=[
            pltpu.VMEM((batch, channels), BF16),
            pltpu.VMEM((1, channels), F32),
            pltpu.SemaphoreType.DMA((2,)),
        ],
        compiler_params=params(8),
        cost_estimate=cost(10 * tokens.size, 2 * n_gx * tokens.size),
    )(in_hbm(tokens), in_hbm(gain.reshape(1, -1)))


def assemble_kernel(gy_ref, rows_ref, after_ref, out_ref):
    del after_ref
    devices, batch, _ = rows_ref.shape
    quarter = devices // 4
    pack = 16 // batch
    for at, turn in enumerate(ORDER):
        base = (gy_ref[0] ^ turn) * quarter
        for i in range(0, quarter, pack):
            tall = jnp.concatenate(
                [rows_ref[base + i + k].astype(F32) for k in range(pack)], axis=0
            )
            start = (at * quarter + i) * batch
            out_ref[start : start + 16] = tall.astype(BF16)


def assemble(gy, rows, after):
    devices, batch, width = rows.shape
    return pl.pallas_call(
        assemble_kernel,
        in_specs=[SCALARS, WHOLE, ANYWHERE],
        out_specs=WHOLE,
        out_shape=vmem_out((devices * batch, width), BF16),
        compiler_params=params(4),
        cost_estimate=cost(2 * rows.size, 4 * rows.size),
    )(gy, in_vmem(rows), after)


def spread_rows(out_ref, value, gy, columns=slice(None)):
    devices, batch, _ = out_ref.shape
    quarter = devices // 4
    for at, turn in enumerate(ORDER):
        base = (gy ^ turn) * quarter
        for i in range(quarter):
            start = (at * quarter + i) * batch
            out_ref[base + i, :, columns] = value[start : start + batch].astype(out_ref.dtype)


def gate_up_tile(x, weights, at, tile, keep_ref, send_ref):
    half = keep_ref.shape[1]
    for k, weight in enumerate(weights):
        value = jnp.dot(x, weight, preferred_element_type=F32)
        keep_ref[k, :, at : at + tile] = value[:half]
        send_ref[k, :, at : at + tile] = value[half:].astype(BF16)


def gate_up_kernel(start, tile, x_ref, gate_ref, up_ref, after_ref, keep_ref, send_ref, slots, sems):
    del after_ref
    width = keep_ref.shape[2]
    depth = x_ref.shape[1]
    copies = []
    for at in range(0, width, tile):
        for k, source in enumerate((gate_ref, up_ref)):
            copies.append(
                pltpu.make_async_copy(
                    source.at[:, pl.ds(start + at, tile)],
                    slots.at[k, at // tile],
                    sems.at[k, at // tile],
                )
            )
    for copy in copies:
        copy.start()
    x = x_ref[...]
    for n in range(width // tile):
        for k in range(2):
            copies[2 * n + k].wait()
        gate_up_tile(x, [slots[k, n] for k in range(2)], n * tile, tile, keep_ref, send_ref)


def gate_up_shapes(rows, width):
    half = rows // 2
    return [
        vmem_out((2, half, width), F32),
        vmem_out((2, half, width), BF16),
    ]


def gate_up(x, w_gate, w_up, start, width, after):
    rows, depth = x.shape
    tile = tile_of(width, 256)
    count = width // tile
    return pl.pallas_call(
        functools.partial(gate_up_kernel, start, tile),
        in_specs=[WHOLE, ANYWHERE, ANYWHERE, ANYWHERE],
        out_specs=[WHOLE, WHOLE],
        out_shape=gate_up_shapes(rows, width),
        scratch_shapes=[
            pltpu.VMEM((2, count, depth, tile), BF16),
            pltpu.SemaphoreType.DMA((2, count)),
        ],
        compiler_params=params(22),
        cost_estimate=cost(rows * depth * width, depth * width),
    )(in_vmem(x), in_hbm(w_gate), in_hbm(w_up), after)


def down_kernel(start, tile, has_sum, last, gy_ref, *refs):
    hidden, (weight_ref, *refs) = refs[:4], refs[4:]
    sum_ref = refs.pop(0) if has_sum else None
    out_ref, slots, sems = refs
    depth = hidden[0].shape[1]
    width = weight_ref.shape[1]
    copies = [
        pltpu.make_async_copy(
            weight_ref.at[pl.ds(start, depth), pl.ds(at, tile)],
            slots.at[at // tile],
            sems.at[at // tile],
        )
        for at in range(0, width, tile)
    ]
    for copy in copies:
        copy.start()
    x = jnp.concatenate([h[...] for h in hidden], axis=0)
    gy = gy_ref[0]
    for n, copy in enumerate(copies):
        columns = slice(n * tile, (n + 1) * tile)
        copy.wait()
        value = jnp.dot(x, slots[n], preferred_element_type=F32)
        if has_sum:
            value = value + sum_ref[:, columns]
        if last:
            spread_rows(out_ref, value, gy, columns)
        else:
            out_ref[:, columns] = value


def down(gy, hidden, w_down, start, total, devices, last):
    part_rows, depth = hidden[0].shape
    rows = 4 * part_rows
    width = w_down.shape[1]
    tile = tile_of(width, 256)
    count = width // tile
    args = [gy, *[in_vmem(h) for h in hidden], in_hbm(w_down)]
    in_specs = [SCALARS] + [WHOLE] * 4 + [ANYWHERE]
    if total is not None:
        args.append(in_vmem(total))
        in_specs.append(WHOLE)
    shape = (devices, rows // devices, width) if last else (rows, width)
    return pl.pallas_call(
        functools.partial(down_kernel, start, tile, total is not None, last),
        in_specs=in_specs,
        out_specs=WHOLE,
        out_shape=vmem_out(shape, BF16 if last else F32),
        scratch_shapes=[
            pltpu.VMEM((count, depth, tile), BF16),
            pltpu.SemaphoreType.DMA((count,)),
        ],
        compiler_params=params(22),
        cost_estimate=cost(rows * depth * width, depth * width),
    )(*args)


def finish_kernel(tokens_ref, sums_ref, out_ref):
    sources, blocks, _, width = sums_ref.shape
    for b in range(blocks):
        columns = slice(b * width, (b + 1) * width)
        ffn = sums_ref[0, b].astype(F32)
        for s in range(1, sources):
            ffn = ffn + sums_ref[s, b].astype(F32)
        out_ref[:, columns] = (tokens_ref[:, columns].astype(F32) + ffn).astype(BF16)


def finish(tokens, sums):
    return pl.pallas_call(
        finish_kernel,
        in_specs=[WHOLE, WHOLE],
        out_specs=WHOLE,
        out_shape=jax.ShapeDtypeStruct(tokens.shape, BF16),
        compiler_params=params(8),
        cost_estimate=cost(sums.size, 2 * sums.size),
    )(in_vmem(tokens), in_vmem(sums))


def fresh_kernel(gy_ref, x_ref, weight_ref, after_ref, out_ref):
    del after_ref
    value = jnp.dot(x_ref[...], weight_ref[0], preferred_element_type=F32)
    spread_rows(out_ref, value, gy_ref[0])


def fresh_part(gy, x, w_kv, devices, after):
    rows, depth = x.shape
    columns = w_kv.shape[2]
    return pl.pallas_call(
        fresh_kernel,
        in_specs=[SCALARS, WHOLE, WHOLE, ANYWHERE],
        out_specs=WHOLE,
        out_shape=vmem_out((devices, rows // devices, columns), F32),
        compiler_params=params(8),
        cost_estimate=cost(2 * rows * depth * columns, 2 * depth * columns),
    )(gy, in_vmem(x), in_vmem(w_kv), after)


def cache_kernel(
    scale, lengths_ref, query_ref, key_ref, value_ref, after_ref,
    acc_ref, top_ref, sum_ref, keys, values, cache_sems,
):
    del after_ref
    batch = query_ref.shape[0]
    caches = [
        [
            pltpu.make_async_copy(source.at[r], slots.at[r], cache_sems.at[k, r])
            for k, (source, slots) in enumerate(((key_ref, keys), (value_ref, values)))
        ]
        for r in range(batch)
    ]
    for pair in caches:
        for copy in pair:
            copy.start()
    for r in range(batch):
        caches[r][0].wait()
        scores = scale * lax.dot_general(
            query_ref[r], keys[r], (((1,), (1,)), ((), ())), preferred_element_type=F32
        )
        heads = scores.shape[0]
        live = lax.broadcasted_iota(jnp.int32, scores.shape, 1) < lengths_ref[r]
        scores = jnp.where(live, scores, -jnp.inf)
        top = jnp.max(scores, axis=1, keepdims=True)
        chance = jnp.exp(scores - top)
        high = chance.astype(BF16)
        low = (chance - high.astype(F32)).astype(BF16)
        caches[r][1].wait()
        both = jnp.dot(
            jnp.concatenate((high, low), axis=0), values[r], preferred_element_type=F32
        )
        acc_ref[r] = both[:heads] + both[heads:]
        top_ref[r] = top
        sum_ref[r] = jnp.sum(chance, axis=1, keepdims=True)


def attend_cache(grouped, key_cache, value_cache, lengths, after):
    batch, heads, depth = grouped.shape
    span = key_cache.shape[1]
    return pl.pallas_call(
        functools.partial(cache_kernel, 1.0 / math.sqrt(depth)),
        in_specs=[SCALARS, WHOLE] + [ANYWHERE] * 3,
        out_specs=[WHOLE] * 3,
        out_shape=[
            vmem_out((batch, heads, depth), F32),
            vmem_out((batch, heads, 1), F32),
            vmem_out((batch, heads, 1), F32),
        ],
        scratch_shapes=[
            pltpu.VMEM((batch, span, depth), BF16),
            pltpu.VMEM((batch, span, depth), BF16),
            pltpu.SemaphoreType.DMA((2, batch)),
        ],
        compiler_params=params(16),
        cost_estimate=cost(
            6 * batch * heads * span * depth, 4 * batch * span * depth, batch * heads * span
        ),
    )(lengths, in_vmem(grouped), in_hbm(key_cache), in_hbm(value_cache), after)


def attend_new(grouped, cached, key_new, value_new):
    acc, top_cached, sum_cached = cached
    batch = grouped.shape[0]
    scale = 1.0 / math.sqrt(grouped.shape[2])
    own = jnp.einsum("rhd,rd->rh", grouped, key_new, preferred_element_type=F32)
    own = own[:, :, None] * scale
    top = jnp.maximum(top_cached, own)
    old = jnp.exp(top_cached - top)
    new = jnp.exp(own - top)
    total = sum_cached * old + new
    context = (acc * old + new * value_new.astype(F32)[:, None, :]) / total
    return context.astype(BF16).reshape(batch, -1)


def chunk_widths(columns):
    unit = 256 if columns % 256 == 0 else 128
    units = columns // unit
    side = max(1, 5 * units // 18)
    return [unit * u for u in (side, units - 2 * side, side)]


def body(n_gx, n_gy, tokens, gain, w_gate, w_up, w_down, w_kv, queries, key_cache, value_cache, lengths):
    gx = lax.axis_index("gx")
    gy = lax.axis_index("gy").astype(jnp.int32).reshape(1)
    swap_gy = lambda x, bits: swap(x, "gy", n_gy, bits)
    exchange = lambda x: lax.all_to_all(x, ("gx", "gy"), split_axis=0, concat_axis=0, tiled=True)
    devices = n_gx * n_gy
    batch = tokens.shape[0]
    widths = chunk_widths(w_gate.shape[1])

    normed = norm(tokens, gain, n_gx, n_gy)
    gathered = exchange(normed.reshape(devices, batch, -1))
    grouped = queries.reshape(batch, -1, HD)
    cached = attend_cache(grouped, key_cache, value_cache, lengths, normed)
    x = assemble(gy, gathered, cached[0])
    rows = x.shape[0]
    quarter = rows // 4

    sums = []
    start = 0
    for c, width in enumerate(widths):
        keep, send = gate_up(x, w_gate, w_up, start, width, sums[-1][2] if c else gy)
        core = swap_gy(send, 1)
        across = (keep[:, quarter:] + core[:, quarter:].astype(F32)).astype(BF16)
        sums.append((keep, core, across))
        start += width

    slab = w_kv.shape[1]
    part = fresh_part(gy, lax.dynamic_slice_in_dim(x, gx * slab, slab, 1), w_kv, devices, send)
    fresh = jnp.sum(exchange(part), axis=0)
    key_new = fresh[:, :HD].astype(BF16)
    value_new = fresh[:, HD:].astype(BF16)

    start = 0
    total = None
    for c, (keep, core, across) in enumerate(sums):
        pair = keep[:, :quarter] + core[:, :quarter].astype(F32) + swap_gy(across, 2).astype(F32)
        own = (jax.nn.silu(pair[0]) * pair[1]).astype(BF16)
        far = swap_gy(own, 2)
        hidden = (own, far, swap_gy(own, 1), swap_gy(far, 1))
        total = down(gy, hidden, w_down, start, total, devices, c == len(sums) - 1)
        start += widths[c]

    ffn = exchange(total)
    mixed = finish(tokens, ffn.reshape(n_gx, n_gy, batch, -1))
    context = attend_new(grouped, cached, key_new, value_new)
    return (mixed, context)


def solution(mesh):
    sizes = dict(mesh.shape)
    return jax.shard_map(
        functools.partial(body, sizes["gx"], sizes["gy"]),
        mesh=mesh,
        in_specs=(
            P(("gx", "gy"), None),
            P(),
            P("gy", "gx"),
            P("gy", "gx"),
            P("gx", "gy"),
            P("gy", "gx", None),
            P(("gx", "gy"), None),
            P(("gx", "gy"), None, None),
            P(("gx", "gy"), None, None),
            P(("gx", "gy")),
        ),
        out_specs=(P(("gx", "gy"), None), P(("gx", "gy"), None)),
        check_vma=False,
    )
```

```python
import functools
import math

import jax
import jax.numpy as jnp
from jax import lax
from jax.experimental import pallas as pl
from jax.experimental.pallas import tpu as pltpu
from jax.sharding import PartitionSpec as P

HD = 256
F32 = jnp.float32
BF16 = jnp.bfloat16
MIB = 1024 * 1024
WHOLE = pl.BlockSpec(memory_space=pltpu.VMEM)
SCALARS = pl.BlockSpec(memory_space=pltpu.SMEM)
ANYWHERE = pl.BlockSpec(memory_space=pl.ANY)
ORDER = (0, 2, 1, 3)


def params(mib):
    return pltpu.CompilerParams(vmem_limit_bytes=mib * MIB)


def cost(flops, moved, transcendentals=0):
    return pl.CostEstimate(flops=flops, bytes_accessed=moved, transcendentals=transcendentals)


def tile_of(width, most):
    return max(t for t in range(128, most + 1, 128) if width % t == 0)


def in_hbm(x):
    return pltpu.with_memory_space_constraint(x, pltpu.HBM)


def hbm_out(shape, dtype):
    return pltpu.HBM(shape, dtype)


def vmem_out(shape, dtype):
    return pltpu.VMEM(shape, dtype)


def in_vmem(x):
    return pltpu.with_memory_space_constraint(x, pltpu.VMEM)


def swap(x, axis, size, bits):
    return lax.ppermute(x, axis, [(i, i ^ bits) for i in range(size)])


def norm_kernel(tokens_hbm, gain_hbm, *refs):
    *out_refs, tokens_ref, gain_ref, sems = refs
    copies, blocks = out_refs[0].shape[:2]
    width = sum(ref.shape[3] for ref in out_refs)
    moves = [
        pltpu.make_async_copy(source, target, sems.at[k])
        for k, (source, target) in enumerate(((tokens_hbm, tokens_ref), (gain_hbm, gain_ref)))
    ]
    for move in moves:
        move.start()
    for move in moves:
        move.wait()
    values = tokens_ref[...].astype(F32)
    centred = values - jnp.mean(values, axis=-1, keepdims=True)
    spread = jnp.mean(centred * centred, axis=-1, keepdims=True)
    normed = (centred * lax.rsqrt(spread + 1e-05) * gain_ref[...]).astype(BF16)
    for b in range(blocks):
        start = b * width
        for out_ref in out_refs:
            part = normed[:, start : start + out_ref.shape[3]]
            start += out_ref.shape[3]
            for c in range(copies):
                out_ref[c, b] = part


def norm(tokens, gain, n_gx, n_gy, widths):
    batch, channels = tokens.shape
    return pl.pallas_call(
        norm_kernel,
        in_specs=[ANYWHERE, ANYWHERE],
        out_specs=[WHOLE] * len(widths),
        out_shape=[vmem_out((n_gx, n_gy, batch, width), BF16) for width in widths],
        scratch_shapes=[
            pltpu.VMEM((batch, channels), BF16),
            pltpu.VMEM((1, channels), F32),
            pltpu.SemaphoreType.DMA((2,)),
        ],
        compiler_params=params(8),
        cost_estimate=cost(10 * tokens.size, 2 * n_gx * tokens.size),
    )(in_hbm(tokens), in_hbm(gain.reshape(1, -1)))


def assemble_kernel(gy_ref, rows_ref, *refs):
    out_ref = refs[-1]
    first = 0
    if len(refs) > 1:
        first = refs[0].shape[1]
        out_ref[:, :first] = refs[0][...]
    devices, batch, _ = rows_ref.shape
    quarter = devices // 4
    pack = 16 // batch
    for at, turn in enumerate(ORDER):
        base = (gy_ref[0] ^ turn) * quarter
        for i in range(0, quarter, pack):
            tall = jnp.concatenate(
                [rows_ref[base + i + k].astype(F32) for k in range(pack)], axis=0
            )
            start = (at * quarter + i) * batch
            out_ref[start : start + 16, first:] = tall.astype(BF16)


def assemble(gy, rows, before=(), after=()):
    devices, batch, width = rows.shape
    width += sum(x.shape[1] for x in before)
    return pl.pallas_call(
        assemble_kernel,
        in_specs=[SCALARS, WHOLE] + [WHOLE] * len(before) + [ANYWHERE] * len(after),
        out_specs=WHOLE,
        out_shape=vmem_out((devices * batch, width), BF16),
        compiler_params=params(4),
        cost_estimate=cost(2 * rows.size, 4 * rows.size),
    )(gy, in_vmem(rows), *[in_vmem(x) for x in before], *after)


def spread_rows(out_ref, value, gy, columns=slice(None)):
    devices, batch, _ = out_ref.shape
    quarter = devices // 4
    for at, turn in enumerate(ORDER):
        base = (gy ^ turn) * quarter
        for i in range(quarter):
            start = (at * quarter + i) * batch
            out_ref[base + i, :, columns] = value[start : start + batch].astype(out_ref.dtype)


def in_turn(groups, ahead):
    for group in groups[:ahead]:
        for copy in group:
            copy.start()
    for n, group in enumerate(groups):
        for copy in group:
            copy.wait()
        if n + ahead < len(groups):
            for copy in groups[n + ahead]:
                copy.start()
        yield n


def gate_up_first_kernel(tile, x_ref, gate_ref, up_ref, out_ref, slots, sums, sems, out_sems):
    depth = x_ref.shape[1]
    groups = []
    outs = []
    for n in range(slots.shape[1]):
        columns = pl.ds(n * tile, tile)
        groups.append(
            [
                pltpu.make_async_copy(
                    source.at[pl.ds(0, depth), columns], slots.at[k, n], sems.at[k, n]
                )
                for k, source in enumerate((gate_ref, up_ref))
            ]
        )
        outs.append(
            pltpu.make_async_copy(sums.at[n], out_ref.at[:, :, columns], out_sems.at[n])
        )
    x = x_ref[...]
    for n in in_turn(groups, 3):
        for k in range(2):
            sums[n, k] = jnp.dot(x, slots[k, n], preferred_element_type=F32)
        outs[n].start()
    for out in outs:
        out.wait()


def gate_up_first(x, w_gate, w_up):
    rows, depth = x.shape
    width = w_gate.shape[1]
    tile = tile_of(width, 256)
    count = width // tile
    return pl.pallas_call(
        functools.partial(gate_up_first_kernel, tile),
        in_specs=[WHOLE, ANYWHERE, ANYWHERE],
        out_specs=ANYWHERE,
        out_shape=hbm_out((2, rows, width), F32),
        scratch_shapes=[
            pltpu.VMEM((2, count, depth, tile), BF16),
            pltpu.VMEM((count, 2, rows, tile), F32),
            pltpu.SemaphoreType.DMA((2, count)),
            pltpu.SemaphoreType.DMA((count,)),
        ],
        compiler_params=params(28),
        cost_estimate=cost(4 * rows * depth * width, 4 * depth * width),
    )(in_vmem(x), in_hbm(w_gate), in_hbm(w_up))


def gate_up_kernel(start, tile, first, count_after, x_ref, gate_ref, up_ref, sums_ref, *refs):
    keep_ref, send_ref, slots, sum_slots, sems = refs[count_after:]
    _, half, width = keep_ref.shape
    depth = slots.shape[2]
    groups = []
    for n in range(width // tile):
        columns = pl.ds(start + n * tile, tile)
        groups.append(
            [
                pltpu.make_async_copy(
                    source.at[pl.ds(first, depth), columns], slots.at[k, n], sems.at[k, n]
                )
                for k, source in enumerate((gate_ref, up_ref))
            ]
            + [pltpu.make_async_copy(sums_ref.at[:, :, columns], sum_slots.at[n], sems.at[2, n])]
        )
    x = x_ref[:, first:]
    for n in in_turn(groups, 3):
        columns = slice(n * tile, (n + 1) * tile)
        for k in range(2):
            value = jnp.dot(x, slots[k, n], preferred_element_type=F32) + sum_slots[n, k]
            keep_ref[k, :, columns] = value[:half]
            send_ref[k, :, columns] = value[half:].astype(BF16)


def gate_up(x, w_gate, w_up, sums, first, start, width, after):
    rows = x.shape[0]
    depth = x.shape[1] - first
    half = rows // 2
    tile = tile_of(width, 256)
    count = width // tile
    return pl.pallas_call(
        functools.partial(gate_up_kernel, start, tile, first, len(after)),
        in_specs=[WHOLE] + [ANYWHERE] * (3 + len(after)),
        out_specs=[WHOLE, WHOLE],
        out_shape=[vmem_out((2, half, width), F32), vmem_out((2, half, width), BF16)],
        scratch_shapes=[
            pltpu.VMEM((2, count, depth, tile), BF16),
            pltpu.VMEM((count, 2, rows, tile), F32),
            pltpu.SemaphoreType.DMA((3, count)),
        ],
        compiler_params=params(20),
        cost_estimate=cost(rows * depth * width, depth * width),
    )(in_vmem(x), in_hbm(w_gate), in_hbm(w_up), in_hbm(sums), *after)


def combine_kernel(keep_ref, core_ref, own_ref, across_ref):
    half = own_ref.shape[1]
    own_ref[...] = keep_ref[:, :half] + core_ref[:, :half].astype(F32)
    across_ref[...] = (keep_ref[:, half:] + core_ref[:, half:].astype(F32)).astype(BF16)


def combine(keep, core):
    _, half, width = keep.shape
    shape = (2, half // 2, width)
    return pl.pallas_call(
        combine_kernel,
        in_specs=[WHOLE, WHOLE],
        out_specs=[WHOLE, WHOLE],
        out_shape=[vmem_out(shape, F32), vmem_out(shape, BF16)],
        compiler_params=params(4),
        cost_estimate=cost(keep.size, keep.size),
    )(in_vmem(keep), in_vmem(core))


def activate_kernel(own_ref, far_ref, *refs):
    gate = own_ref[0] + far_ref[0].astype(F32)
    up = own_ref[1] + far_ref[1].astype(F32)
    refs[-1][...] = (jax.nn.silu(gate) * up).astype(BF16)


def activate(own, far, after):
    return pl.pallas_call(
        activate_kernel,
        in_specs=[WHOLE, WHOLE] + [ANYWHERE] * len(after),
        out_specs=WHOLE,
        out_shape=vmem_out(own.shape[1:], BF16),
        compiler_params=params(4),
        cost_estimate=cost(own.size, own.size),
    )(in_vmem(own), in_vmem(far), *after)


def down_kernel(start, tile, has_sum, last, gy_ref, *refs):
    hidden, (weight_ref, *refs) = refs[:4], refs[4:]
    sum_ref = refs.pop(0) if has_sum else None
    out_ref, slots, sems = refs[-3:]
    depth = hidden[0].shape[1]
    width = weight_ref.shape[1]
    groups = [
        [
            pltpu.make_async_copy(
                weight_ref.at[pl.ds(start, depth), pl.ds(n * tile, tile)],
                slots.at[n],
                sems.at[n],
            )
        ]
        for n in range(width // tile)
    ]
    x = jnp.concatenate([h[...] for h in hidden], axis=0)
    gy = gy_ref[0]
    for n in in_turn(groups, 5):
        columns = slice(n * tile, (n + 1) * tile)
        value = jnp.dot(x, slots[n], preferred_element_type=F32)
        if has_sum:
            value = value + sum_ref[:, columns]
        if last:
            spread_rows(out_ref, value, gy, columns)
        else:
            out_ref[:, columns] = value


def down(gy, hidden, w_down, start, total, devices, last, after):
    part_rows, depth = hidden[0].shape
    rows = 4 * part_rows
    width = w_down.shape[1]
    tile = tile_of(width, 256)
    count = width // tile
    args = [gy, *[in_vmem(h) for h in hidden], in_hbm(w_down)]
    in_specs = [SCALARS] + [WHOLE] * 4 + [ANYWHERE]
    if total is not None:
        args.append(in_vmem(total))
        in_specs.append(WHOLE)
    args.extend(after)
    in_specs.extend([ANYWHERE] * len(after))
    shape = (devices, rows // devices, width) if last else (rows, width)
    return pl.pallas_call(
        functools.partial(down_kernel, start, tile, total is not None, last),
        in_specs=in_specs,
        out_specs=WHOLE,
        out_shape=vmem_out(shape, BF16 if last else F32),
        scratch_shapes=[
            pltpu.VMEM((count, depth, tile), BF16),
            pltpu.SemaphoreType.DMA((count,)),
        ],
        compiler_params=params(22),
        cost_estimate=cost(rows * depth * width, depth * width),
    )(*args)


def finish_kernel(tokens_ref, sums_ref, out_ref):
    sources, blocks, _, width = sums_ref.shape
    for b in range(blocks):
        columns = slice(b * width, (b + 1) * width)
        ffn = sums_ref[0, b].astype(F32)
        for s in range(1, sources):
            ffn = ffn + sums_ref[s, b].astype(F32)
        out_ref[:, columns] = (tokens_ref[:, columns].astype(F32) + ffn).astype(BF16)


def finish(tokens, sums):
    return pl.pallas_call(
        finish_kernel,
        in_specs=[WHOLE, WHOLE],
        out_specs=WHOLE,
        out_shape=jax.ShapeDtypeStruct(tokens.shape, BF16),
        compiler_params=params(8),
        cost_estimate=cost(sums.size, 2 * sums.size),
    )(in_vmem(tokens), in_vmem(sums))


def fresh_kernel(gy_ref, x_ref, weight_ref, after_ref, out_ref):
    del after_ref
    value = jnp.dot(x_ref[...], weight_ref[0], preferred_element_type=F32)
    spread_rows(out_ref, value, gy_ref[0])


def fresh_part(gy, x, w_kv, devices, after):
    rows, depth = x.shape
    columns = w_kv.shape[2]
    return pl.pallas_call(
        fresh_kernel,
        in_specs=[SCALARS, WHOLE, WHOLE, ANYWHERE],
        out_specs=WHOLE,
        out_shape=vmem_out((devices, rows // devices, columns), F32),
        compiler_params=params(8),
        cost_estimate=cost(2 * rows * depth * columns, 2 * depth * columns),
    )(gy, in_vmem(x), in_vmem(w_kv), after)


def cache_kernel(
    scale, lengths_ref, query_ref, key_ref, value_ref, after_ref,
    acc_ref, top_ref, sum_ref, keys, values, cache_sems,
):
    del after_ref
    batch = query_ref.shape[0]
    caches = [
        [
            pltpu.make_async_copy(source.at[r], slots.at[r], cache_sems.at[k, r])
            for k, (source, slots) in enumerate(((key_ref, keys), (value_ref, values)))
        ]
        for r in range(batch)
    ]
    for pair in caches:
        for copy in pair:
            copy.start()
    for r in range(batch):
        caches[r][0].wait()
        scores = scale * lax.dot_general(
            query_ref[r], keys[r], (((1,), (1,)), ((), ())), preferred_element_type=F32
        )
        heads = scores.shape[0]
        live = lax.broadcasted_iota(jnp.int32, scores.shape, 1) < lengths_ref[r]
        scores = jnp.where(live, scores, -jnp.inf)
        top = jnp.max(scores, axis=1, keepdims=True)
        chance = jnp.exp(scores - top)
        high = chance.astype(BF16)
        low = (chance - high.astype(F32)).astype(BF16)
        caches[r][1].wait()
        both = jnp.dot(
            jnp.concatenate((high, low), axis=0), values[r], preferred_element_type=F32
        )
        acc_ref[r] = both[:heads] + both[heads:]
        top_ref[r] = top
        sum_ref[r] = jnp.sum(chance, axis=1, keepdims=True)


def attend_cache(grouped, key_cache, value_cache, lengths, after):
    batch, heads, depth = grouped.shape
    span = key_cache.shape[1]
    return pl.pallas_call(
        functools.partial(cache_kernel, 1.0 / math.sqrt(depth)),
        in_specs=[SCALARS, WHOLE] + [ANYWHERE] * 3,
        out_specs=[WHOLE] * 3,
        out_shape=[
            vmem_out((batch, heads, depth), F32),
            vmem_out((batch, heads, 1), F32),
            vmem_out((batch, heads, 1), F32),
        ],
        scratch_shapes=[
            pltpu.VMEM((batch, span, depth), BF16),
            pltpu.VMEM((batch, span, depth), BF16),
            pltpu.SemaphoreType.DMA((2, batch)),
        ],
        compiler_params=params(16),
        cost_estimate=cost(
            6 * batch * heads * span * depth, 4 * batch * span * depth, batch * heads * span
        ),
    )(lengths, in_vmem(grouped), in_hbm(key_cache), in_hbm(value_cache), after)


def attend_new(grouped, cached, key_new, value_new):
    acc, top_cached, sum_cached = cached
    batch = grouped.shape[0]
    scale = 1.0 / math.sqrt(grouped.shape[2])
    own = jnp.einsum("rhd,rd->rh", grouped, key_new, preferred_element_type=F32)
    own = own[:, :, None] * scale
    top = jnp.maximum(top_cached, own)
    old = jnp.exp(top_cached - top)
    new = jnp.exp(own - top)
    total = sum_cached * old + new
    context = (acc * old + new * value_new.astype(F32)[:, None, :]) / total
    return context.astype(BF16).reshape(batch, -1)


def chunk_widths(columns):
    unit = 256 if columns % 256 == 0 else 128
    units = columns // unit
    side = max(1, 5 * units // 18)
    return [unit * u for u in (side, units - 2 * side, side)]


def body(n_gx, n_gy, tokens, gain, w_gate, w_up, w_down, w_kv, queries, key_cache, value_cache, lengths):
    gx = lax.axis_index("gx")
    gy = lax.axis_index("gy").astype(jnp.int32).reshape(1)
    swap_gy = lambda x, bits: swap(x, "gy", n_gy, bits)
    exchange = lambda x: lax.all_to_all(x, ("gx", "gy"), split_axis=0, concat_axis=0, tiled=True)
    devices = n_gx * n_gy
    batch = tokens.shape[0]
    widths = chunk_widths(w_gate.shape[1])

    depth = w_gate.shape[0]
    unit = 256 if depth % 256 == 0 else 128
    first = depth // unit // 2 * unit

    normed = norm(tokens, gain, n_gx, n_gy, (first, depth - first))
    parts = [exchange(part.reshape(devices, batch, -1)) for part in normed]
    x_first = assemble(gy, parts[0])
    sums = gate_up_first(x_first, w_gate, w_up)
    x = assemble(gy, parts[1], [x_first], [sums])

    owns, far, hidden = [], [], []
    start = 0
    after = []
    for c, width in enumerate(widths):
        keep, send = gate_up(x, w_gate, w_up, sums, first, start, width, after)
        own, across = combine(keep, swap_gy(send, 1))
        owns.append(own)
        far.append(swap_gy(across, 2))
        after = [across]
        if c == 1:
            hidden.append(activate(owns[0], far[0], []))
            after.append(hidden[0])
        start += width
    hidden.append(activate(owns[1], far[1], [across]))

    slab = w_kv.shape[1]
    part = fresh_part(gy, lax.dynamic_slice_in_dim(x, gx * slab, slab, 1), w_kv, devices, across)
    fresh = jnp.sum(exchange(part), axis=0)
    key_new = fresh[:, :HD].astype(BF16)
    value_new = fresh[:, HD:].astype(BF16)

    total = None
    start = 0
    for c, width in enumerate(widths):
        if c == 1:
            hidden.append(activate(owns[2], far[2], [total]))
        own = hidden[c]
        other = swap_gy(own, 2)
        pieces = (own, other, swap_gy(own, 1), swap_gy(other, 1))
        last = c == len(widths) - 1
        total = down(gy, pieces, w_down, start, total, devices, last, [] if last else [hidden[c + 1]])
        start += width

    ffn = exchange(total)
    grouped = queries.reshape(batch, -1, HD)
    cached = attend_cache(grouped, key_cache, value_cache, lengths, total)
    context = attend_new(grouped, cached, key_new, value_new)
    mixed = finish(tokens, ffn.reshape(n_gx, n_gy, batch, -1))
    return (mixed, context)


def solution(mesh):
    sizes = dict(mesh.shape)
    return jax.shard_map(
        functools.partial(body, sizes["gx"], sizes["gy"]),
        mesh=mesh,
        in_specs=(
            P(("gx", "gy"), None),
            P(),
            P("gy", "gx"),
            P("gy", "gx"),
            P("gx", "gy"),
            P("gy", "gx", None),
            P(("gx", "gy"), None),
            P(("gx", "gy"), None, None),
            P(("gx", "gy"), None, None),
            P(("gx", "gy")),
        ),
        out_specs=(P(("gx", "gy"), None), P(("gx", "gy"), None)),
        check_vma=False,
    )
```

```python
import functools
import math

import jax
import jax.numpy as jnp
from jax import lax
from jax.experimental import pallas as pl
from jax.experimental.pallas import tpu as pltpu
from jax.sharding import PartitionSpec as P

HD = 256
F32 = jnp.float32
BF16 = jnp.bfloat16
MIB = 1024 * 1024
WHOLE = pl.BlockSpec(memory_space=pltpu.VMEM)
SCALARS = pl.BlockSpec(memory_space=pltpu.SMEM)
ANYWHERE = pl.BlockSpec(memory_space=pl.ANY)
ORDER = (0, 2, 1, 3)


def params(mib):
    return pltpu.CompilerParams(vmem_limit_bytes=mib * MIB)


def cost(flops, moved, transcendentals=0):
    return pl.CostEstimate(flops=flops, bytes_accessed=moved, transcendentals=transcendentals)


def tile_of(width, most):
    return max(t for t in range(128, most + 1, 128) if width % t == 0)


def in_hbm(x):
    return pltpu.with_memory_space_constraint(x, pltpu.HBM)


def hbm_out(shape, dtype):
    return pltpu.HBM(shape, dtype)


def vmem_out(shape, dtype):
    return pltpu.VMEM(shape, dtype)


def in_vmem(x):
    return pltpu.with_memory_space_constraint(x, pltpu.VMEM)


def swap(x, axis, size, bits):
    return lax.ppermute(x, axis, [(i, i ^ bits) for i in range(size)])


def norm_kernel(tokens_hbm, gain_hbm, *refs):
    *out_refs, tokens_ref, gain_ref, sems = refs
    copies, blocks = out_refs[0].shape[:2]
    width = sum(ref.shape[3] for ref in out_refs)
    moves = [
        pltpu.make_async_copy(source, target, sems.at[k])
        for k, (source, target) in enumerate(((tokens_hbm, tokens_ref), (gain_hbm, gain_ref)))
    ]
    for move in moves:
        move.start()
    for move in moves:
        move.wait()
    values = tokens_ref[...].astype(F32)
    centred = values - jnp.mean(values, axis=-1, keepdims=True)
    spread = jnp.mean(centred * centred, axis=-1, keepdims=True)
    normed = (centred * lax.rsqrt(spread + 1e-05) * gain_ref[...]).astype(BF16)
    for b in range(blocks):
        start = b * width
        for out_ref in out_refs:
            part = normed[:, start : start + out_ref.shape[3]]
            start += out_ref.shape[3]
            for c in range(copies):
                out_ref[c, b] = part


def norm(tokens, gain, n_gx, n_gy, widths):
    batch, channels = tokens.shape
    return pl.pallas_call(
        norm_kernel,
        in_specs=[ANYWHERE, ANYWHERE],
        out_specs=[WHOLE] * len(widths),
        out_shape=[vmem_out((n_gx, n_gy, batch, width), BF16) for width in widths],
        scratch_shapes=[
            pltpu.VMEM((batch, channels), BF16),
            pltpu.VMEM((1, channels), F32),
            pltpu.SemaphoreType.DMA((2,)),
        ],
        compiler_params=params(8),
        cost_estimate=cost(10 * tokens.size, 2 * n_gx * tokens.size),
    )(in_hbm(tokens), in_hbm(gain.reshape(1, -1)))


def assemble_kernel(gy_ref, rows_ref, after_ref, out_ref):
    del after_ref
    devices, batch, _ = rows_ref.shape
    quarter = devices // 4
    pack = 16 // batch
    for at, turn in enumerate(ORDER):
        base = (gy_ref[0] ^ turn) * quarter
        for i in range(0, quarter, pack):
            tall = jnp.concatenate(
                [rows_ref[base + i + k].astype(F32) for k in range(pack)], axis=0
            )
            start = (at * quarter + i) * batch
            out_ref[start : start + 16] = tall.astype(BF16)


def assemble(gy, rows, after):
    devices, batch, width = rows.shape
    return pl.pallas_call(
        assemble_kernel,
        in_specs=[SCALARS, WHOLE, ANYWHERE],
        out_specs=WHOLE,
        out_shape=vmem_out((devices * batch, width), BF16),
        compiler_params=params(4),
        cost_estimate=cost(2 * rows.size, 4 * rows.size),
    )(gy, in_vmem(rows), after)


def spread_rows(out_ref, value, gy, columns=slice(None)):
    devices, batch, _ = out_ref.shape
    quarter = devices // 4
    for at, turn in enumerate(ORDER):
        base = (gy ^ turn) * quarter
        for i in range(quarter):
            start = (at * quarter + i) * batch
            out_ref[base + i, :, columns] = value[start : start + batch].astype(out_ref.dtype)


def tie_kernel(*refs):
    del refs


def tie(x, after):
    return pl.pallas_call(
        tie_kernel,
        in_specs=[ANYWHERE] * (1 + len(after)),
        out_specs=ANYWHERE,
        out_shape=jax.ShapeDtypeStruct(x.shape, x.dtype),
        input_output_aliases={0: 0},
        compiler_params=params(1),
        cost_estimate=cost(0, 0),
    )(x, *after)


def in_turn(groups, ahead):
    for group in groups[:ahead]:
        for copy in group:
            copy.start()
    for n, group in enumerate(groups):
        for copy in group:
            copy.wait()
        if n + ahead < len(groups):
            for copy in groups[n + ahead]:
                copy.start()
        yield n


def gate_up_kernel(start, tile, count_after, x_ref, gate_ref, up_ref, *refs):
    keep_ref, send_ref, slots, sems = refs[count_after:]
    _, half, width = keep_ref.shape
    groups = []
    for n in range(width // tile):
        columns = pl.ds(start + n * tile, tile)
        groups.append(
            [
                pltpu.make_async_copy(source.at[:, columns], slots.at[k, n], sems.at[k, n])
                for k, source in enumerate((gate_ref, up_ref))
            ]
        )
    x = x_ref[...]
    for n in in_turn(groups, 3):
        columns = slice(n * tile, (n + 1) * tile)
        for k in range(2):
            value = jnp.dot(x, slots[k, n], preferred_element_type=F32)
            keep_ref[k, :, columns] = value[:half]
            send_ref[k, :, columns] = value[half:].astype(BF16)


def gate_up(x, w_gate, w_up, start, width, after):
    rows, depth = x.shape
    half = rows // 2
    tile = tile_of(width, 256)
    count = width // tile
    return pl.pallas_call(
        functools.partial(gate_up_kernel, start, tile, len(after)),
        in_specs=[WHOLE] + [ANYWHERE] * (2 + len(after)),
        out_specs=[WHOLE, WHOLE],
        out_shape=[vmem_out((2, half, width), F32), vmem_out((2, half, width), BF16)],
        scratch_shapes=[
            pltpu.VMEM((2, count, depth, tile), BF16),
            pltpu.SemaphoreType.DMA((2, count)),
        ],
        compiler_params=params(22),
        cost_estimate=cost(rows * depth * width, depth * width),
    )(in_vmem(x), in_hbm(w_gate), in_hbm(w_up), *after)


def combine_kernel(keep_ref, core_ref, own_ref, across_ref):
    half = own_ref.shape[1]
    own_ref[...] = keep_ref[:, :half] + core_ref[:, :half].astype(F32)
    across_ref[...] = (keep_ref[:, half:] + core_ref[:, half:].astype(F32)).astype(BF16)


def combine(keep, core):
    _, half, width = keep.shape
    shape = (2, half // 2, width)
    return pl.pallas_call(
        combine_kernel,
        in_specs=[WHOLE, WHOLE],
        out_specs=[WHOLE, WHOLE],
        out_shape=[vmem_out(shape, F32), vmem_out(shape, BF16)],
        compiler_params=params(4),
        cost_estimate=cost(keep.size, keep.size),
    )(in_vmem(keep), in_vmem(core))


def activate_kernel(own_ref, far_ref, *refs):
    gate = own_ref[0] + far_ref[0].astype(F32)
    up = own_ref[1] + far_ref[1].astype(F32)
    refs[-1][...] = (jax.nn.silu(gate) * up).astype(BF16)


def activate(own, far, after):
    return pl.pallas_call(
        activate_kernel,
        in_specs=[WHOLE, WHOLE] + [ANYWHERE] * len(after),
        out_specs=WHOLE,
        out_shape=vmem_out(own.shape[1:], BF16),
        compiler_params=params(4),
        cost_estimate=cost(own.size, own.size),
    )(in_vmem(own), in_vmem(far), *after)


def down_kernel(start, tile, has_sum, last, gy_ref, *refs):
    hidden, (weight_ref, *refs) = refs[:4], refs[4:]
    sum_ref = refs.pop(0) if has_sum else None
    out_ref, slots, sems = refs[-3:]
    depth = hidden[0].shape[1]
    width = weight_ref.shape[1]
    groups = [
        [
            pltpu.make_async_copy(
                weight_ref.at[pl.ds(start, depth), pl.ds(n * tile, tile)],
                slots.at[n],
                sems.at[n],
            )
        ]
        for n in range(width // tile)
    ]
    x = jnp.concatenate([h[...] for h in hidden], axis=0)
    gy = gy_ref[0]
    for n in in_turn(groups, 5):
        columns = slice(n * tile, (n + 1) * tile)
        value = jnp.dot(x, slots[n], preferred_element_type=F32)
        if has_sum:
            value = value + sum_ref[:, columns]
        if last:
            spread_rows(out_ref, value, gy, columns)
        else:
            out_ref[:, columns] = value


def down(gy, hidden, w_down, start, total, devices, last, after):
    part_rows, depth = hidden[0].shape
    rows = 4 * part_rows
    width = w_down.shape[1]
    tile = tile_of(width, 256)
    count = width // tile
    args = [gy, *[in_vmem(h) for h in hidden], in_hbm(w_down)]
    in_specs = [SCALARS] + [WHOLE] * 4 + [ANYWHERE]
    if total is not None:
        args.append(in_vmem(total))
        in_specs.append(WHOLE)
    args.extend(after)
    in_specs.extend([ANYWHERE] * len(after))
    shape = (devices, rows // devices, width) if last else (rows, width)
    return pl.pallas_call(
        functools.partial(down_kernel, start, tile, total is not None, last),
        in_specs=in_specs,
        out_specs=WHOLE,
        out_shape=vmem_out(shape, BF16 if last else F32),
        scratch_shapes=[
            pltpu.VMEM((count, depth, tile), BF16),
            pltpu.SemaphoreType.DMA((count,)),
        ],
        compiler_params=params(22),
        cost_estimate=cost(rows * depth * width, depth * width),
    )(*args)


def finish_kernel(tokens_ref, sums_ref, out_ref):
    sources, blocks, _, width = sums_ref.shape
    for b in range(blocks):
        columns = slice(b * width, (b + 1) * width)
        ffn = sums_ref[0, b].astype(F32)
        for s in range(1, sources):
            ffn = ffn + sums_ref[s, b].astype(F32)
        out_ref[:, columns] = (tokens_ref[:, columns].astype(F32) + ffn).astype(BF16)


def finish(tokens, sums):
    return pl.pallas_call(
        finish_kernel,
        in_specs=[WHOLE, WHOLE],
        out_specs=WHOLE,
        out_shape=jax.ShapeDtypeStruct(tokens.shape, BF16),
        compiler_params=params(8),
        cost_estimate=cost(sums.size, 2 * sums.size),
    )(in_vmem(tokens), in_vmem(sums))


def fresh_kernel(gy_ref, x_ref, weight_ref, after_ref, out_ref):
    del after_ref
    value = jnp.dot(x_ref[...], weight_ref[0], preferred_element_type=F32)
    spread_rows(out_ref, value, gy_ref[0])


def fresh_part(gy, x, w_kv, devices, after):
    rows, depth = x.shape
    columns = w_kv.shape[2]
    return pl.pallas_call(
        fresh_kernel,
        in_specs=[SCALARS, WHOLE, WHOLE, ANYWHERE],
        out_specs=WHOLE,
        out_shape=vmem_out((devices, rows // devices, columns), F32),
        compiler_params=params(8),
        cost_estimate=cost(2 * rows * depth * columns, 2 * depth * columns),
    )(gy, in_vmem(x), in_vmem(w_kv), after)


def cache_kernel(
    scale, lengths_ref, query_ref, key_ref, value_ref, after_ref,
    acc_ref, top_ref, sum_ref, keys, values, cache_sems,
):
    del after_ref
    batch = query_ref.shape[0]
    caches = [
        [
            pltpu.make_async_copy(source.at[r], slots.at[r], cache_sems.at[k, r])
            for k, (source, slots) in enumerate(((key_ref, keys), (value_ref, values)))
        ]
        for r in range(batch)
    ]
    for pair in caches:
        for copy in pair:
            copy.start()
    for r in range(batch):
        caches[r][0].wait()
        scores = scale * lax.dot_general(
            query_ref[r], keys[r], (((1,), (1,)), ((), ())), preferred_element_type=F32
        )
        heads = scores.shape[0]
        live = lax.broadcasted_iota(jnp.int32, scores.shape, 1) < lengths_ref[r]
        scores = jnp.where(live, scores, -jnp.inf)
        top = jnp.max(scores, axis=1, keepdims=True)
        chance = jnp.exp(scores - top)
        high = chance.astype(BF16)
        low = (chance - high.astype(F32)).astype(BF16)
        caches[r][1].wait()
        both = jnp.dot(
            jnp.concatenate((high, low), axis=0), values[r], preferred_element_type=F32
        )
        acc_ref[r] = both[:heads] + both[heads:]
        top_ref[r] = top
        sum_ref[r] = jnp.sum(chance, axis=1, keepdims=True)


def attend_cache(grouped, key_cache, value_cache, lengths, after):
    batch, heads, depth = grouped.shape
    span = key_cache.shape[1]
    return pl.pallas_call(
        functools.partial(cache_kernel, 1.0 / math.sqrt(depth)),
        in_specs=[SCALARS, WHOLE] + [ANYWHERE] * 3,
        out_specs=[WHOLE] * 3,
        out_shape=[
            vmem_out((batch, heads, depth), F32),
            vmem_out((batch, heads, 1), F32),
            vmem_out((batch, heads, 1), F32),
        ],
        scratch_shapes=[
            pltpu.VMEM((batch, span, depth), BF16),
            pltpu.VMEM((batch, span, depth), BF16),
            pltpu.SemaphoreType.DMA((2, batch)),
        ],
        compiler_params=params(16),
        cost_estimate=cost(
            6 * batch * heads * span * depth, 4 * batch * span * depth, batch * heads * span
        ),
    )(lengths, in_vmem(grouped), in_hbm(key_cache), in_hbm(value_cache), after)


def attend_new(grouped, cached, key_new, value_new):
    acc, top_cached, sum_cached = cached
    batch = grouped.shape[0]
    scale = 1.0 / math.sqrt(grouped.shape[2])
    own = jnp.einsum("rhd,rd->rh", grouped, key_new, preferred_element_type=F32)
    own = own[:, :, None] * scale
    top = jnp.maximum(top_cached, own)
    old = jnp.exp(top_cached - top)
    new = jnp.exp(own - top)
    total = sum_cached * old + new
    context = (acc * old + new * value_new.astype(F32)[:, None, :]) / total
    return context.astype(BF16).reshape(batch, -1)


def chunk_widths(columns):
    unit = 256 if columns % 256 == 0 else 128
    units = columns // unit
    side = max(1, 5 * units // 18)
    return [unit * u for u in (side, units - 2 * side, side)]


def body(n_gx, n_gy, tokens, gain, w_gate, w_up, w_down, w_kv, queries, key_cache, value_cache, lengths):
    gx = lax.axis_index("gx")
    gy = lax.axis_index("gy").astype(jnp.int32).reshape(1)
    swap_gy = lambda x, bits: swap(x, "gy", n_gy, bits)
    exchange = lambda x: lax.all_to_all(x, ("gx", "gy"), split_axis=0, concat_axis=0, tiled=True)
    devices = n_gx * n_gy
    batch = tokens.shape[0]
    widths = chunk_widths(w_gate.shape[1])

    (normed,) = norm(tokens, gain, n_gx, n_gy, (w_gate.shape[0],))
    gathered = exchange(normed.reshape(devices, batch, -1))
    grouped = queries.reshape(batch, -1, HD)
    cached = attend_cache(grouped, key_cache, value_cache, lengths, normed)
    x = assemble(gy, gathered, cached[0])

    starts = [sum(widths[:c]) for c in range(len(widths))]

    def project(c, after):
        return gate_up(x, w_gate, w_up, starts[c], widths[c], after)

    def back(c, own, after):
        other = tie(swap_gy(own, 2), after)
        return own, other, swap_gy(own, 1), swap_gy(other, 1)

    def through(c, pieces, total, after):
        last = c == len(widths) - 1
        return down(gy, pieces, w_down, starts[c], total, devices, last, after)

    keep, send = project(0, [])
    own_0, across_0 = combine(keep, swap_gy(send, 1))
    far_0 = swap_gy(across_0, 2)
    keep, send = project(1, [across_0])
    hidden_0 = activate(own_0, far_0, [send])
    own_1, across_1 = combine(keep, swap_gy(tie(send, [hidden_0]), 1))
    far_1 = swap_gy(across_1, 2)
    keep, send = project(2, [across_1])
    pieces_0 = back(0, hidden_0, [send])
    own_2, across_2 = combine(keep, swap_gy(send, 1))
    far_2 = swap_gy(across_2, 2)
    hidden_1 = activate(own_1, far_1, [across_2])

    slab = w_kv.shape[1]
    part = fresh_part(gy, lax.dynamic_slice_in_dim(x, gx * slab, slab, 1), w_kv, devices, send)
    fresh = jnp.sum(exchange(tie(part, [across_2])), axis=0)
    key_new = fresh[:, :HD].astype(BF16)
    value_new = fresh[:, HD:].astype(BF16)

    total = through(0, pieces_0, None, [hidden_1])
    pieces_1 = back(1, hidden_1, [total])
    hidden_2 = activate(own_2, far_2, [total])
    total = through(1, pieces_1, total, [hidden_2])
    pieces_2 = back(2, hidden_2, [total])
    total = through(2, pieces_2, total, [])

    ffn = exchange(total)
    context = attend_new(grouped, cached, key_new, value_new)
    mixed = finish(tokens, ffn.reshape(n_gx, n_gy, batch, -1))
    return (mixed, context)


def solution(mesh):
    sizes = dict(mesh.shape)
    return jax.shard_map(
        functools.partial(body, sizes["gx"], sizes["gy"]),
        mesh=mesh,
        in_specs=(
            P(("gx", "gy"), None),
            P(),
            P("gy", "gx"),
            P("gy", "gx"),
            P("gx", "gy"),
            P("gy", "gx", None),
            P(("gx", "gy"), None),
            P(("gx", "gy"), None, None),
            P(("gx", "gy"), None, None),
            P(("gx", "gy")),
        ),
        out_specs=(P(("gx", "gy"), None), P(("gx", "gy"), None)),
        check_vma=False,
    )
```

```python
import functools
import math

import jax
import jax.numpy as jnp
from jax import lax
from jax.experimental import pallas as pl
from jax.experimental.pallas import tpu as pltpu
from jax.sharding import PartitionSpec as P

HD = 256
F32 = jnp.float32
BF16 = jnp.bfloat16
MIB = 1024 * 1024
WHOLE = pl.BlockSpec(memory_space=pltpu.VMEM)
SCALARS = pl.BlockSpec(memory_space=pltpu.SMEM)
ANYWHERE = pl.BlockSpec(memory_space=pl.ANY)
ORDER = (0, 2, 1, 3)


def params(mib):
    return pltpu.CompilerParams(vmem_limit_bytes=mib * MIB)


def cost(flops, moved, transcendentals=0):
    return pl.CostEstimate(flops=flops, bytes_accessed=moved, transcendentals=transcendentals)


def tile_of(width, most):
    return max(t for t in range(128, most + 1, 128) if width % t == 0)


def in_hbm(x):
    return pltpu.with_memory_space_constraint(x, pltpu.HBM)


def hbm_out(shape, dtype):
    return pltpu.HBM(shape, dtype)


def vmem_out(shape, dtype):
    return pltpu.VMEM(shape, dtype)


def in_vmem(x):
    return pltpu.with_memory_space_constraint(x, pltpu.VMEM)


def swap(x, axis, size, bits):
    return lax.ppermute(x, axis, [(i, i ^ bits) for i in range(size)])


def norm_kernel(tokens_hbm, gain_hbm, *refs):
    *out_refs, tokens_ref, gain_ref, sems = refs
    copies, blocks = out_refs[0].shape[:2]
    width = sum(ref.shape[3] for ref in out_refs)
    moves = [
        pltpu.make_async_copy(source, target, sems.at[k])
        for k, (source, target) in enumerate(((tokens_hbm, tokens_ref), (gain_hbm, gain_ref)))
    ]
    for move in moves:
        move.start()
    for move in moves:
        move.wait()
    values = tokens_ref[...].astype(F32)
    centred = values - jnp.mean(values, axis=-1, keepdims=True)
    spread = jnp.mean(centred * centred, axis=-1, keepdims=True)
    normed = (centred * lax.rsqrt(spread + 1e-05) * gain_ref[...]).astype(BF16)
    for b in range(blocks):
        start = b * width
        for out_ref in out_refs:
            part = normed[:, start : start + out_ref.shape[3]]
            start += out_ref.shape[3]
            for c in range(copies):
                out_ref[c, b] = part


def norm(tokens, gain, n_gx, n_gy, widths):
    batch, channels = tokens.shape
    return pl.pallas_call(
        norm_kernel,
        in_specs=[ANYWHERE, ANYWHERE],
        out_specs=[WHOLE] * len(widths),
        out_shape=[vmem_out((n_gx, n_gy, batch, width), BF16) for width in widths],
        scratch_shapes=[
            pltpu.VMEM((batch, channels), BF16),
            pltpu.VMEM((1, channels), F32),
            pltpu.SemaphoreType.DMA((2,)),
        ],
        compiler_params=params(8),
        cost_estimate=cost(10 * tokens.size, 2 * n_gx * tokens.size),
    )(in_hbm(tokens), in_hbm(gain.reshape(1, -1)))


def assemble_kernel(gy_ref, rows_ref, after_ref, out_ref):
    del after_ref
    devices, batch, _ = rows_ref.shape
    quarter = devices // 4
    pack = 16 // batch
    for at, turn in enumerate(ORDER):
        base = (gy_ref[0] ^ turn) * quarter
        for i in range(0, quarter, pack):
            tall = jnp.concatenate(
                [rows_ref[base + i + k].astype(F32) for k in range(pack)], axis=0
            )
            start = (at * quarter + i) * batch
            out_ref[start : start + 16] = tall.astype(BF16)


def assemble(gy, rows, after):
    devices, batch, width = rows.shape
    return pl.pallas_call(
        assemble_kernel,
        in_specs=[SCALARS, WHOLE, ANYWHERE],
        out_specs=WHOLE,
        out_shape=vmem_out((devices * batch, width), BF16),
        compiler_params=params(4),
        cost_estimate=cost(2 * rows.size, 4 * rows.size),
    )(gy, in_vmem(rows), after)


def spread_rows(out_ref, value, gy, columns=slice(None)):
    devices, batch, _ = out_ref.shape
    quarter = devices // 4
    for at, turn in enumerate(ORDER):
        base = (gy ^ turn) * quarter
        for i in range(quarter):
            start = (at * quarter + i) * batch
            out_ref[base + i, :, columns] = value[start : start + batch].astype(out_ref.dtype)


def tie_kernel(*refs):
    del refs


def tie(x, after):
    return pl.pallas_call(
        tie_kernel,
        in_specs=[ANYWHERE] * (1 + len(after)),
        out_specs=ANYWHERE,
        out_shape=jax.ShapeDtypeStruct(x.shape, x.dtype),
        input_output_aliases={0: 0},
        compiler_params=params(1),
        cost_estimate=cost(0, 0),
    )(x, *after)


def in_turn(groups, ahead):
    for group in groups[:ahead]:
        for copy in group:
            copy.start()
    for n, group in enumerate(groups):
        for copy in group:
            copy.wait()
        if n + ahead < len(groups):
            for copy in groups[n + ahead]:
                copy.start()
        yield n


def gate_up_kernel(start, tile, count_after, x_ref, gate_ref, up_ref, *refs):
    keep_ref, send_ref, slots, sems = refs[count_after:]
    _, half, width = keep_ref.shape
    groups = []
    for n in range(width // tile):
        columns = pl.ds(start + n * tile, tile)
        groups.append(
            [
                pltpu.make_async_copy(source.at[:, columns], slots.at[k, n], sems.at[k, n])
                for k, source in enumerate((gate_ref, up_ref))
            ]
        )
    x = x_ref[...]
    for n in in_turn(groups, 3):
        columns = slice(n * tile, (n + 1) * tile)
        for k in range(2):
            value = jnp.dot(x, slots[k, n], preferred_element_type=F32)
            keep_ref[k, :, columns] = value[:half]
            send_ref[k, :, columns] = value[half:].astype(BF16)


def gate_up(x, w_gate, w_up, start, width, after):
    rows, depth = x.shape
    half = rows // 2
    tile = tile_of(width, 256)
    count = width // tile
    return pl.pallas_call(
        functools.partial(gate_up_kernel, start, tile, len(after)),
        in_specs=[WHOLE] + [ANYWHERE] * (2 + len(after)),
        out_specs=[WHOLE, WHOLE],
        out_shape=[vmem_out((2, half, width), F32), vmem_out((2, half, width), BF16)],
        scratch_shapes=[
            pltpu.VMEM((2, count, depth, tile), BF16),
            pltpu.SemaphoreType.DMA((2, count)),
        ],
        compiler_params=params(22),
        cost_estimate=cost(rows * depth * width, depth * width),
    )(in_vmem(x), in_hbm(w_gate), in_hbm(w_up), *after)


def combine_kernel(keep_ref, core_ref, own_ref, across_ref):
    half = own_ref.shape[1]
    own_ref[...] = keep_ref[:, :half] + core_ref[:, :half].astype(F32)
    across_ref[...] = (keep_ref[:, half:] + core_ref[:, half:].astype(F32)).astype(BF16)


def combine(keep, core):
    _, half, width = keep.shape
    shape = (2, half // 2, width)
    return pl.pallas_call(
        combine_kernel,
        in_specs=[WHOLE, WHOLE],
        out_specs=[WHOLE, WHOLE],
        out_shape=[vmem_out(shape, F32), vmem_out(shape, BF16)],
        compiler_params=params(4),
        cost_estimate=cost(keep.size, keep.size),
    )(in_vmem(keep), in_vmem(core))


def activate_kernel(own_ref, far_ref, *refs):
    gate = own_ref[0] + far_ref[0].astype(F32)
    up = own_ref[1] + far_ref[1].astype(F32)
    refs[-1][...] = (jax.nn.silu(gate) * up).astype(BF16)


def activate(own, far, after):
    return pl.pallas_call(
        activate_kernel,
        in_specs=[WHOLE, WHOLE] + [ANYWHERE] * len(after),
        out_specs=WHOLE,
        out_shape=vmem_out(own.shape[1:], BF16),
        compiler_params=params(4),
        cost_estimate=cost(own.size, own.size),
    )(in_vmem(own), in_vmem(far), *after)


def down_kernel(start, tile, has_sum, last, gy_ref, *refs):
    hidden, (weight_ref, *refs) = refs[:4], refs[4:]
    out_ref = refs[-1]
    depth = hidden[0].shape[1]
    x = jnp.concatenate([h[...] for h in hidden], axis=0)
    gy = gy_ref[0]
    for at in range(0, weight_ref.shape[1], tile):
        columns = slice(at, at + tile)
        value = jnp.dot(
            x, weight_ref[start : start + depth, columns], preferred_element_type=F32
        )
        if has_sum:
            value = value + refs[0][:, columns]
        if last:
            spread_rows(out_ref, value, gy, columns)
        else:
            out_ref[:, columns] = value


def down(gy, hidden, w_down, start, total, devices, last, after):
    part_rows, depth = hidden[0].shape
    rows = 4 * part_rows
    width = w_down.shape[1]
    args = [gy, *[in_vmem(h) for h in hidden], in_vmem(w_down)]
    in_specs = [SCALARS] + [WHOLE] * 5
    if total is not None:
        args.append(in_vmem(total))
        in_specs.append(WHOLE)
    args.extend(after)
    in_specs.extend([ANYWHERE] * len(after))
    shape = (devices, rows // devices, width) if last else (rows, width)
    return pl.pallas_call(
        functools.partial(down_kernel, start, tile_of(width, 256), total is not None, last),
        in_specs=in_specs,
        out_specs=WHOLE,
        out_shape=vmem_out(shape, BF16 if last else F32),
        compiler_params=params(8),
        cost_estimate=cost(rows * depth * width, depth * width),
    )(*args)


def finish_kernel(tokens_ref, sums_ref, out_ref):
    sources, blocks, _, width = sums_ref.shape
    for b in range(blocks):
        columns = slice(b * width, (b + 1) * width)
        ffn = sums_ref[0, b].astype(F32)
        for s in range(1, sources):
            ffn = ffn + sums_ref[s, b].astype(F32)
        out_ref[:, columns] = (tokens_ref[:, columns].astype(F32) + ffn).astype(BF16)


def finish(tokens, sums):
    return pl.pallas_call(
        finish_kernel,
        in_specs=[WHOLE, WHOLE],
        out_specs=WHOLE,
        out_shape=jax.ShapeDtypeStruct(tokens.shape, BF16),
        compiler_params=params(8),
        cost_estimate=cost(sums.size, 2 * sums.size),
    )(in_vmem(tokens), in_vmem(sums))


def fresh_kernel(gy_ref, x_ref, weight_ref, after_ref, out_ref):
    del after_ref
    value = jnp.dot(x_ref[...], weight_ref[0], preferred_element_type=F32)
    spread_rows(out_ref, value, gy_ref[0])


def fresh_part(gy, x, w_kv, devices, after):
    rows, depth = x.shape
    columns = w_kv.shape[2]
    return pl.pallas_call(
        fresh_kernel,
        in_specs=[SCALARS, WHOLE, WHOLE, ANYWHERE],
        out_specs=WHOLE,
        out_shape=vmem_out((devices, rows // devices, columns), F32),
        compiler_params=params(8),
        cost_estimate=cost(2 * rows * depth * columns, 2 * depth * columns),
    )(gy, in_vmem(x), in_vmem(w_kv), after)


def cache_kernel(
    scale, lengths_ref, query_ref, key_ref, value_ref, after_ref,
    acc_ref, top_ref, sum_ref, keys, values, cache_sems,
):
    del after_ref
    batch = query_ref.shape[0]
    caches = [
        [
            pltpu.make_async_copy(source.at[r], slots.at[r], cache_sems.at[k, r])
            for k, (source, slots) in enumerate(((key_ref, keys), (value_ref, values)))
        ]
        for r in range(batch)
    ]
    for pair in caches:
        for copy in pair:
            copy.start()
    for r in range(batch):
        caches[r][0].wait()
        scores = scale * lax.dot_general(
            query_ref[r], keys[r], (((1,), (1,)), ((), ())), preferred_element_type=F32
        )
        heads = scores.shape[0]
        live = lax.broadcasted_iota(jnp.int32, scores.shape, 1) < lengths_ref[r]
        scores = jnp.where(live, scores, -jnp.inf)
        top = jnp.max(scores, axis=1, keepdims=True)
        chance = jnp.exp(scores - top)
        high = chance.astype(BF16)
        low = (chance - high.astype(F32)).astype(BF16)
        caches[r][1].wait()
        both = jnp.dot(
            jnp.concatenate((high, low), axis=0), values[r], preferred_element_type=F32
        )
        acc_ref[r] = both[:heads] + both[heads:]
        top_ref[r] = top
        sum_ref[r] = jnp.sum(chance, axis=1, keepdims=True)


def attend_cache(grouped, key_cache, value_cache, lengths, after):
    batch, heads, depth = grouped.shape
    span = key_cache.shape[1]
    return pl.pallas_call(
        functools.partial(cache_kernel, 1.0 / math.sqrt(depth)),
        in_specs=[SCALARS, WHOLE] + [ANYWHERE] * 3,
        out_specs=[WHOLE] * 3,
        out_shape=[
            vmem_out((batch, heads, depth), F32),
            vmem_out((batch, heads, 1), F32),
            vmem_out((batch, heads, 1), F32),
        ],
        scratch_shapes=[
            pltpu.VMEM((batch, span, depth), BF16),
            pltpu.VMEM((batch, span, depth), BF16),
            pltpu.SemaphoreType.DMA((2, batch)),
        ],
        compiler_params=params(16),
        cost_estimate=cost(
            6 * batch * heads * span * depth, 4 * batch * span * depth, batch * heads * span
        ),
    )(lengths, in_vmem(grouped), in_hbm(key_cache), in_hbm(value_cache), after)


def attend_new(grouped, cached, key_new, value_new):
    acc, top_cached, sum_cached = cached
    batch = grouped.shape[0]
    scale = 1.0 / math.sqrt(grouped.shape[2])
    own = jnp.einsum("rhd,rd->rh", grouped, key_new, preferred_element_type=F32)
    own = own[:, :, None] * scale
    top = jnp.maximum(top_cached, own)
    old = jnp.exp(top_cached - top)
    new = jnp.exp(own - top)
    total = sum_cached * old + new
    context = (acc * old + new * value_new.astype(F32)[:, None, :]) / total
    return context.astype(BF16).reshape(batch, -1)


def chunk_widths(columns):
    unit = 256 if columns % 256 == 0 else 128
    units = columns // unit
    side = max(1, 5 * units // 18)
    return [unit * u for u in (side, units - 2 * side, side)]


def body(n_gx, n_gy, tokens, gain, w_gate, w_up, w_down, w_kv, queries, key_cache, value_cache, lengths):
    gx = lax.axis_index("gx")
    gy = lax.axis_index("gy").astype(jnp.int32).reshape(1)
    swap_gy = lambda x, bits: swap(x, "gy", n_gy, bits)
    exchange = lambda x: lax.all_to_all(x, ("gx", "gy"), split_axis=0, concat_axis=0, tiled=True)
    devices = n_gx * n_gy
    batch = tokens.shape[0]
    widths = chunk_widths(w_gate.shape[1])

    (normed,) = norm(tokens, gain, n_gx, n_gy, (w_gate.shape[0],))
    gathered = exchange(normed.reshape(devices, batch, -1))
    grouped = queries.reshape(batch, -1, HD)
    cached = attend_cache(grouped, key_cache, value_cache, lengths, normed)
    x = assemble(gy, gathered, cached[0])

    starts = [sum(widths[:c]) for c in range(len(widths))]

    def project(c, after):
        return gate_up(x, w_gate, w_up, starts[c], widths[c], after)

    def back(c, own, after):
        other = tie(swap_gy(own, 2), after)
        return own, other, swap_gy(own, 1), swap_gy(other, 1)

    def through(c, pieces, total, after):
        last = c == len(widths) - 1
        return down(gy, pieces, w_down, starts[c], total, devices, last, after)

    keep, send = project(0, [])
    own_0, across_0 = combine(keep, swap_gy(send, 1))
    far_0 = swap_gy(across_0, 2)
    keep, send = project(1, [across_0])
    hidden_0 = activate(own_0, far_0, [send])
    own_1, across_1 = combine(keep, swap_gy(tie(send, [hidden_0]), 1))
    far_1 = swap_gy(across_1, 2)
    keep, send = project(2, [across_1])
    hidden_1 = activate(own_1, far_1, [send])
    pieces_0 = back(0, hidden_0, [send])
    own_2, across_2 = combine(keep, swap_gy(tie(send, [hidden_1, pieces_0[1]]), 1))
    far_2 = swap_gy(across_2, 2)

    total = through(0, pieces_0, None, [across_2])
    pieces_1 = back(1, hidden_1, [total])
    hidden_2 = activate(own_2, far_2, [total])

    slab = w_kv.shape[1]
    part = fresh_part(gy, lax.dynamic_slice_in_dim(x, gx * slab, slab, 1), w_kv, devices, send)
    fresh = jnp.sum(exchange(tie(part, [hidden_2])), axis=0)
    key_new = fresh[:, :HD].astype(BF16)
    value_new = fresh[:, HD:].astype(BF16)

    total = through(1, pieces_1, total, [hidden_2])
    pieces_2 = back(2, hidden_2, [total])
    total = through(2, pieces_2, total, [])

    ffn = exchange(total)
    context = attend_new(grouped, cached, key_new, value_new)
    mixed = finish(tokens, ffn.reshape(n_gx, n_gy, batch, -1))
    return (mixed, context)


def solution(mesh):
    sizes = dict(mesh.shape)
    return jax.shard_map(
        functools.partial(body, sizes["gx"], sizes["gy"]),
        mesh=mesh,
        in_specs=(
            P(("gx", "gy"), None),
            P(),
            P("gy", "gx"),
            P("gy", "gx"),
            P("gx", "gy"),
            P("gy", "gx", None),
            P(("gx", "gy"), None),
            P(("gx", "gy"), None, None),
            P(("gx", "gy"), None, None),
            P(("gx", "gy")),
        ),
        out_specs=(P(("gx", "gy"), None), P(("gx", "gy"), None)),
        check_vma=False,
    )
```

```python
import functools
import math

import jax
import jax.numpy as jnp
from jax import lax
from jax.experimental import pallas as pl
from jax.experimental.pallas import tpu as pltpu
from jax.sharding import PartitionSpec as P

HD = 256
F32 = jnp.float32
BF16 = jnp.bfloat16
MIB = 1024 * 1024
WHOLE = pl.BlockSpec(memory_space=pltpu.VMEM)
SCALARS = pl.BlockSpec(memory_space=pltpu.SMEM)
ANYWHERE = pl.BlockSpec(memory_space=pl.ANY)
ORDER = (0, 2, 1, 3)


def params(mib):
    return pltpu.CompilerParams(vmem_limit_bytes=mib * MIB)


def cost(flops, moved, transcendentals=0):
    return pl.CostEstimate(flops=flops, bytes_accessed=moved, transcendentals=transcendentals)


def tile_of(width, most):
    return max(t for t in range(128, most + 1, 128) if width % t == 0)


def in_hbm(x):
    return pltpu.with_memory_space_constraint(x, pltpu.HBM)


def hbm_out(shape, dtype):
    return pltpu.HBM(shape, dtype)


def vmem_out(shape, dtype):
    return pltpu.VMEM(shape, dtype)


def in_vmem(x):
    return pltpu.with_memory_space_constraint(x, pltpu.VMEM)


def swap(x, axis, size, bits):
    return lax.ppermute(x, axis, [(i, i ^ bits) for i in range(size)])


def norm_kernel(tokens_hbm, gain_hbm, *refs):
    *out_refs, tokens_ref, gain_ref, sems = refs
    copies, blocks = out_refs[0].shape[:2]
    width = sum(ref.shape[3] for ref in out_refs)
    moves = [
        pltpu.make_async_copy(source, target, sems.at[k])
        for k, (source, target) in enumerate(((tokens_hbm, tokens_ref), (gain_hbm, gain_ref)))
    ]
    for move in moves:
        move.start()
    for move in moves:
        move.wait()
    values = tokens_ref[...].astype(F32)
    centred = values - jnp.mean(values, axis=-1, keepdims=True)
    spread = jnp.mean(centred * centred, axis=-1, keepdims=True)
    normed = (centred * lax.rsqrt(spread + 1e-05) * gain_ref[...]).astype(BF16)
    for b in range(blocks):
        start = b * width
        for out_ref in out_refs:
            part = normed[:, start : start + out_ref.shape[3]]
            start += out_ref.shape[3]
            for c in range(copies):
                out_ref[c, b] = part


def norm(tokens, gain, n_gx, n_gy, widths):
    batch, channels = tokens.shape
    return pl.pallas_call(
        norm_kernel,
        in_specs=[ANYWHERE, ANYWHERE],
        out_specs=[WHOLE] * len(widths),
        out_shape=[vmem_out((n_gx, n_gy, batch, width), BF16) for width in widths],
        scratch_shapes=[
            pltpu.VMEM((batch, channels), BF16),
            pltpu.VMEM((1, channels), F32),
            pltpu.SemaphoreType.DMA((2,)),
        ],
        compiler_params=params(8),
        cost_estimate=cost(10 * tokens.size, 2 * n_gx * tokens.size),
    )(in_hbm(tokens), in_hbm(gain.reshape(1, -1)))


def assemble_kernel(gy_ref, rows_ref, after_ref, out_ref):
    del after_ref
    devices, batch, _ = rows_ref.shape
    quarter = devices // 4
    pack = 16 // batch
    for at, turn in enumerate(ORDER):
        base = (gy_ref[0] ^ turn) * quarter
        for i in range(0, quarter, pack):
            tall = jnp.concatenate(
                [rows_ref[base + i + k].astype(F32) for k in range(pack)], axis=0
            )
            start = (at * quarter + i) * batch
            out_ref[start : start + 16] = tall.astype(BF16)


def assemble(gy, rows, after):
    devices, batch, width = rows.shape
    return pl.pallas_call(
        assemble_kernel,
        in_specs=[SCALARS, WHOLE, ANYWHERE],
        out_specs=WHOLE,
        out_shape=vmem_out((devices * batch, width), BF16),
        compiler_params=params(4),
        cost_estimate=cost(2 * rows.size, 4 * rows.size),
    )(gy, in_vmem(rows), after)


def spread_rows(out_ref, value, gy, columns=slice(None)):
    devices, batch, _ = out_ref.shape
    quarter = devices // 4
    for at, turn in enumerate(ORDER):
        base = (gy ^ turn) * quarter
        for i in range(quarter):
            start = (at * quarter + i) * batch
            out_ref[base + i, :, columns] = value[start : start + batch].astype(out_ref.dtype)


def tie_kernel(*refs):
    del refs


def tie(x, after):
    return pl.pallas_call(
        tie_kernel,
        in_specs=[ANYWHERE] * (1 + len(after)),
        out_specs=ANYWHERE,
        out_shape=jax.ShapeDtypeStruct(x.shape, x.dtype),
        input_output_aliases={0: 0},
        compiler_params=params(1),
        cost_estimate=cost(0, 0),
    )(x, *after)


def in_turn(groups, ahead):
    for group in groups[:ahead]:
        for copy in group:
            copy.start()
    for n, group in enumerate(groups):
        for copy in group:
            copy.wait()
        if n + ahead < len(groups):
            for copy in groups[n + ahead]:
                copy.start()
        yield n


def gate_up_kernel(start, tile, count_after, x_ref, gate_ref, up_ref, *refs):
    keep_ref, send_ref, slots, sems = refs[count_after:]
    _, half, width = keep_ref.shape
    groups = []
    for n in range(width // tile):
        columns = pl.ds(start + n * tile, tile)
        groups.append(
            [
                pltpu.make_async_copy(source.at[:, columns], slots.at[k, n], sems.at[k, n])
                for k, source in enumerate((gate_ref, up_ref))
            ]
        )
    x = x_ref[...]
    for n in in_turn(groups, len(groups)):
        columns = slice(n * tile, (n + 1) * tile)
        for k in range(2):
            value = jnp.dot(x, slots[k, n], preferred_element_type=F32)
            keep_ref[k, :, columns] = value[:half]
            send_ref[k, :, columns] = value[half:].astype(BF16)


def gate_up(x, w_gate, w_up, start, width, after):
    rows, depth = x.shape
    half = rows // 2
    tile = tile_of(width, 256)
    count = width // tile
    return pl.pallas_call(
        functools.partial(gate_up_kernel, start, tile, len(after)),
        in_specs=[WHOLE] + [ANYWHERE] * (2 + len(after)),
        out_specs=[WHOLE, WHOLE],
        out_shape=[vmem_out((2, half, width), F32), vmem_out((2, half, width), BF16)],
        scratch_shapes=[
            pltpu.VMEM((2, count, depth, tile), BF16),
            pltpu.SemaphoreType.DMA((2, count)),
        ],
        compiler_params=params(22),
        cost_estimate=cost(rows * depth * width, depth * width),
    )(in_vmem(x), in_hbm(w_gate), in_hbm(w_up), *after)


def combine_kernel(keep_ref, core_ref, own_ref, across_ref):
    half = own_ref.shape[1]
    own_ref[...] = keep_ref[:, :half] + core_ref[:, :half].astype(F32)
    across_ref[...] = (keep_ref[:, half:] + core_ref[:, half:].astype(F32)).astype(BF16)


def combine(keep, core):
    _, half, width = keep.shape
    shape = (2, half // 2, width)
    return pl.pallas_call(
        combine_kernel,
        in_specs=[WHOLE, WHOLE],
        out_specs=[WHOLE, WHOLE],
        out_shape=[vmem_out(shape, F32), vmem_out(shape, BF16)],
        compiler_params=params(4),
        cost_estimate=cost(keep.size, keep.size),
    )(in_vmem(keep), in_vmem(core))


def activate_kernel(own_ref, far_ref, *refs):
    gate = own_ref[0] + far_ref[0].astype(F32)
    up = own_ref[1] + far_ref[1].astype(F32)
    refs[-1][...] = (jax.nn.silu(gate) * up).astype(BF16)


def activate(own, far, after):
    return pl.pallas_call(
        activate_kernel,
        in_specs=[WHOLE, WHOLE] + [ANYWHERE] * len(after),
        out_specs=WHOLE,
        out_shape=vmem_out(own.shape[1:], BF16),
        compiler_params=params(4),
        cost_estimate=cost(own.size, own.size),
    )(in_vmem(own), in_vmem(far), *after)


def down_kernel(start, tile, has_sum, last, gy_ref, *refs):
    hidden, (weight_ref, *refs) = refs[:4], refs[4:]
    out_ref = refs[-1]
    depth = hidden[0].shape[1]
    x = jnp.concatenate([h[...] for h in hidden], axis=0)
    gy = gy_ref[0]
    for at in range(0, weight_ref.shape[1], tile):
        columns = slice(at, at + tile)
        value = jnp.dot(
            x, weight_ref[start : start + depth, columns], preferred_element_type=F32
        )
        if has_sum:
            value = value + refs[0][:, columns]
        if last:
            spread_rows(out_ref, value, gy, columns)
        else:
            out_ref[:, columns] = value


def down(gy, hidden, w_down, start, total, devices, last, after):
    part_rows, depth = hidden[0].shape
    rows = 4 * part_rows
    width = w_down.shape[1]
    args = [gy, *[in_vmem(h) for h in hidden], in_vmem(w_down)]
    in_specs = [SCALARS] + [WHOLE] * 5
    if total is not None:
        args.append(in_vmem(total))
        in_specs.append(WHOLE)
    args.extend(after)
    in_specs.extend([ANYWHERE] * len(after))
    shape = (devices, rows // devices, width) if last else (rows, width)
    return pl.pallas_call(
        functools.partial(down_kernel, start, tile_of(width, 256), total is not None, last),
        in_specs=in_specs,
        out_specs=WHOLE,
        out_shape=vmem_out(shape, BF16 if last else F32),
        compiler_params=params(8),
        cost_estimate=cost(rows * depth * width, depth * width),
    )(*args)


def finish_kernel(tokens_ref, sums_ref, out_ref):
    sources, blocks, _, width = sums_ref.shape
    for b in range(blocks):
        columns = slice(b * width, (b + 1) * width)
        ffn = sums_ref[0, b].astype(F32)
        for s in range(1, sources):
            ffn = ffn + sums_ref[s, b].astype(F32)
        out_ref[:, columns] = (tokens_ref[:, columns].astype(F32) + ffn).astype(BF16)


def finish(tokens, sums):
    return pl.pallas_call(
        finish_kernel,
        in_specs=[WHOLE, WHOLE],
        out_specs=WHOLE,
        out_shape=jax.ShapeDtypeStruct(tokens.shape, BF16),
        compiler_params=params(8),
        cost_estimate=cost(sums.size, 2 * sums.size),
    )(in_vmem(tokens), in_vmem(sums))


def place_of(q, gx, gy, n_gx):
    blocks = n_gx // 4
    group = gx ^ q
    turn = (group // blocks) ^ gy
    return (((turn & 1) << 1) | (turn >> 1)) * blocks + group % blocks


def fresh_kernel(gx_ref, gy_ref, x_ref, weight_ref, after_ref, near_ref, far_ref, rows_ref):
    del after_ref
    value = jnp.dot(x_ref[...], weight_ref[0], preferred_element_type=F32)
    rows_ref[...] = value.reshape(rows_ref.shape)
    n_gx = rows_ref.shape[0]
    for q in range(n_gx):
        out_ref = (near_ref, far_ref)[q % 2]
        out_ref[q // 2] = rows_ref[place_of(q, gx_ref[0], gy_ref[0], n_gx)]


def fresh_part(gx, gy, x, w_kv, n_gx, after):
    rows, depth = x.shape
    columns = w_kv.shape[2]
    shape = (n_gx // 2, rows // n_gx, columns)
    return pl.pallas_call(
        fresh_kernel,
        in_specs=[SCALARS, SCALARS, WHOLE, WHOLE, ANYWHERE],
        out_specs=[WHOLE, WHOLE],
        out_shape=[vmem_out(shape, F32), vmem_out(shape, F32)],
        scratch_shapes=[pltpu.VMEM((n_gx, rows // n_gx, columns), F32)],
        compiler_params=params(8),
        cost_estimate=cost(2 * rows * depth * columns, 2 * depth * columns),
    )(gx, gy, in_vmem(x), in_vmem(w_kv), after)


def own_first_kernel(gy_ref, sums_ref, near_ref, far_ref):
    for at, turn in enumerate(ORDER):
        (near_ref, far_ref)[at // 2][at % 2] = sums_ref[gy_ref[0] ^ turn]


def own_first(gy, sums):
    shape = (2, *sums.shape[1:])
    return pl.pallas_call(
        own_first_kernel,
        in_specs=[SCALARS, WHOLE],
        out_specs=[WHOLE, WHOLE],
        out_shape=[vmem_out(shape, sums.dtype), vmem_out(shape, sums.dtype)],
        compiler_params=params(4),
        cost_estimate=cost(sums.size, 8 * sums.size),
    )(gy, in_vmem(sums))


def cache_kernel(
    scale, lengths_ref, query_ref, key_ref, value_ref, after_ref,
    acc_ref, top_ref, sum_ref, keys, values, cache_sems,
):
    del after_ref
    batch = query_ref.shape[0]
    caches = [
        [
            pltpu.make_async_copy(source.at[r], slots.at[r], cache_sems.at[k, r])
            for k, (source, slots) in enumerate(((key_ref, keys), (value_ref, values)))
        ]
        for r in range(batch)
    ]
    for pair in caches:
        for copy in pair:
            copy.start()
    for r in range(batch):
        caches[r][0].wait()
        scores = scale * lax.dot_general(
            query_ref[r], keys[r], (((1,), (1,)), ((), ())), preferred_element_type=F32
        )
        heads = scores.shape[0]
        live = lax.broadcasted_iota(jnp.int32, scores.shape, 1) < lengths_ref[r]
        scores = jnp.where(live, scores, -jnp.inf)
        top = jnp.max(scores, axis=1, keepdims=True)
        chance = jnp.exp(scores - top)
        high = chance.astype(BF16)
        low = (chance - high.astype(F32)).astype(BF16)
        caches[r][1].wait()
        both = jnp.dot(
            jnp.concatenate((high, low), axis=0), values[r], preferred_element_type=F32
        )
        acc_ref[r] = both[:heads] + both[heads:]
        top_ref[r] = top
        sum_ref[r] = jnp.sum(chance, axis=1, keepdims=True)


def attend_cache(grouped, key_cache, value_cache, lengths, after):
    batch, heads, depth = grouped.shape
    span = key_cache.shape[1]
    return pl.pallas_call(
        functools.partial(cache_kernel, 1.0 / math.sqrt(depth)),
        in_specs=[SCALARS, WHOLE] + [ANYWHERE] * 3,
        out_specs=[WHOLE] * 3,
        out_shape=[
            vmem_out((batch, heads, depth), F32),
            vmem_out((batch, heads, 1), F32),
            vmem_out((batch, heads, 1), F32),
        ],
        scratch_shapes=[
            pltpu.VMEM((batch, span, depth), BF16),
            pltpu.VMEM((batch, span, depth), BF16),
            pltpu.SemaphoreType.DMA((2, batch)),
        ],
        compiler_params=params(16),
        cost_estimate=cost(
            6 * batch * heads * span * depth, 4 * batch * span * depth, batch * heads * span
        ),
    )(lengths, in_vmem(grouped), in_hbm(key_cache), in_hbm(value_cache), after)


def attend_new(grouped, cached, key_new, value_new):
    acc, top_cached, sum_cached = cached
    batch = grouped.shape[0]
    scale = 1.0 / math.sqrt(grouped.shape[2])
    own = jnp.einsum("rhd,rd->rh", grouped, key_new, preferred_element_type=F32)
    own = own[:, :, None] * scale
    top = jnp.maximum(top_cached, own)
    old = jnp.exp(top_cached - top)
    new = jnp.exp(own - top)
    total = sum_cached * old + new
    context = (acc * old + new * value_new.astype(F32)[:, None, :]) / total
    return context.astype(BF16).reshape(batch, -1)


def chunk_widths(columns):
    unit = 256 if columns % 256 == 0 else 128
    units = columns // unit
    side = max(1, 5 * units // 18)
    return [unit * u for u in (side, units - 2 * side, side)]


def body(n_gx, n_gy, tokens, gain, w_gate, w_up, w_down, w_kv, queries, key_cache, value_cache, lengths):
    gx = lax.axis_index("gx")
    gy = lax.axis_index("gy").astype(jnp.int32).reshape(1)
    gx_row = gx.astype(jnp.int32).reshape(1)
    swap_gx = lambda x, bits: swap(x, "gx", n_gx, bits)
    swap_gy = lambda x, bits: swap(x, "gy", n_gy, bits)
    exchange = lambda x: lax.all_to_all(x, ("gx", "gy"), split_axis=0, concat_axis=0, tiled=True)
    devices = n_gx * n_gy
    batch = tokens.shape[0]
    widths = chunk_widths(w_gate.shape[1])

    (normed,) = norm(tokens, gain, n_gx, n_gy, (w_gate.shape[0],))
    gathered = exchange(normed.reshape(devices, batch, -1))
    grouped = queries.reshape(batch, -1, HD)
    cached = attend_cache(grouped, key_cache, value_cache, lengths, normed)
    x = assemble(gy, gathered, cached[0])

    starts = [sum(widths[:c]) for c in range(len(widths))]

    def project(c, after):
        return gate_up(x, w_gate, w_up, starts[c], widths[c], after)

    def back(c, own, after):
        other = tie(swap_gy(own, 2), after)
        return own, other, swap_gy(own, 1), swap_gy(other, 1)

    def through(c, pieces, total, after):
        last = c == len(widths) - 1
        return down(gy, pieces, w_down, starts[c], total, devices, last, after)

    keep, send = project(0, [])
    slab = w_kv.shape[1]
    near_kv, far_kv = fresh_part(
        gx_row, gy, lax.dynamic_slice_in_dim(x, gx * slab, slab, 1), w_kv, n_gx, send
    )
    far_kv = swap_gx(far_kv, 1)
    own_0, across_0 = combine(keep, swap_gy(send, 1))
    far_0 = swap_gy(across_0, 2)
    keep, send = project(1, [across_0])
    hidden_0 = activate(own_0, far_0, [send])
    near_kv = near_kv + tie(far_kv, [send])
    group_kv = near_kv[0]
    for t in range(1, n_gx // 2):
        group_kv = group_kv + swap_gx(near_kv[t], 2 * t)
    own_1, across_1 = combine(keep, swap_gy(tie(send, [hidden_0]), 1))
    far_1 = swap_gy(across_1, 2)
    keep, send = project(2, [across_1])
    hidden_1 = activate(own_1, far_1, [send])
    pieces_0 = back(0, hidden_0, [send])
    own_2, across_2 = combine(keep, swap_gy(tie(send, [hidden_1, pieces_0[1]]), 1))
    far_2 = swap_gy(across_2, 2)

    hidden_2 = activate(own_2, far_2, [])
    pieces_1 = back(1, tie(hidden_1, [across_2]), [hidden_2])

    own_kv, other_kv = own_first(gy, tie(group_kv, [send]).reshape(n_gy, batch, -1))
    own_kv = own_kv + swap_gy(other_kv, 1)
    fresh = own_kv[0] + swap_gy(tie(own_kv[1], [hidden_2]), 2)
    key_new = fresh[:, :HD].astype(BF16)
    value_new = fresh[:, HD:].astype(BF16)

    total = through(0, pieces_0, None, [hidden_2])
    total = through(1, pieces_1, total, [])
    pieces_2 = back(2, hidden_2, [total])
    total = through(2, pieces_2, total, [])

    ffn = exchange(total)
    context = attend_new(grouped, cached, key_new, value_new)
    mixed = finish(tokens, ffn.reshape(n_gx, n_gy, batch, -1))
    return (mixed, context)


def solution(mesh):
    sizes = dict(mesh.shape)
    return jax.shard_map(
        functools.partial(body, sizes["gx"], sizes["gy"]),
        mesh=mesh,
        in_specs=(
            P(("gx", "gy"), None),
            P(),
            P("gy", "gx"),
            P("gy", "gx"),
            P("gx", "gy"),
            P("gy", "gx", None),
            P(("gx", "gy"), None),
            P(("gx", "gy"), None, None),
            P(("gx", "gy"), None, None),
            P(("gx", "gy")),
        ),
        out_specs=(P(("gx", "gy"), None), P(("gx", "gy"), None)),
        check_vma=False,
    )
```

```python
import functools
import math

import jax
import jax.numpy as jnp
from jax import lax
from jax.experimental import pallas as pl
from jax.experimental.pallas import tpu as pltpu
from jax.sharding import PartitionSpec as P

HD = 256
F32 = jnp.float32
BF16 = jnp.bfloat16
MIB = 1024 * 1024
WHOLE = pl.BlockSpec(memory_space=pltpu.VMEM)
SCALARS = pl.BlockSpec(memory_space=pltpu.SMEM)
ANYWHERE = pl.BlockSpec(memory_space=pl.ANY)
ORDER = (0, 2, 1, 3)


def params(mib):
    return pltpu.CompilerParams(vmem_limit_bytes=mib * MIB)


def cost(flops, moved, transcendentals=0):
    return pl.CostEstimate(flops=flops, bytes_accessed=moved, transcendentals=transcendentals)


def tile_of(width, most):
    return max(t for t in range(128, most + 1, 128) if width % t == 0)


def in_hbm(x):
    return pltpu.with_memory_space_constraint(x, pltpu.HBM)


def hbm_out(shape, dtype):
    return pltpu.HBM(shape, dtype)


def vmem_out(shape, dtype):
    return pltpu.VMEM(shape, dtype)


def in_vmem(x):
    return pltpu.with_memory_space_constraint(x, pltpu.VMEM)


def swap(x, axis, size, bits):
    return lax.ppermute(x, axis, [(i, i ^ bits) for i in range(size)])


def norm_kernel(tokens_hbm, gain_hbm, *refs):
    *out_refs, tokens_ref, gain_ref, sems = refs
    copies, blocks = out_refs[0].shape[:2]
    width = sum(ref.shape[3] for ref in out_refs)
    moves = [
        pltpu.make_async_copy(source, target, sems.at[k])
        for k, (source, target) in enumerate(((tokens_hbm, tokens_ref), (gain_hbm, gain_ref)))
    ]
    for move in moves:
        move.start()
    for move in moves:
        move.wait()
    values = tokens_ref[...].astype(F32)
    centred = values - jnp.mean(values, axis=-1, keepdims=True)
    spread = jnp.mean(centred * centred, axis=-1, keepdims=True)
    normed = (centred * lax.rsqrt(spread + 1e-05) * gain_ref[...]).astype(BF16)
    for b in range(blocks):
        start = b * width
        for out_ref in out_refs:
            part = normed[:, start : start + out_ref.shape[3]]
            start += out_ref.shape[3]
            for c in range(copies):
                out_ref[c, b] = part


def norm(tokens, gain, n_gx, n_gy, widths):
    batch, channels = tokens.shape
    return pl.pallas_call(
        norm_kernel,
        in_specs=[ANYWHERE, ANYWHERE],
        out_specs=[WHOLE] * len(widths),
        out_shape=[vmem_out((n_gx, n_gy, batch, width), BF16) for width in widths],
        scratch_shapes=[
            pltpu.VMEM((batch, channels), BF16),
            pltpu.VMEM((1, channels), F32),
            pltpu.SemaphoreType.DMA((2,)),
        ],
        compiler_params=params(8),
        cost_estimate=cost(10 * tokens.size, 2 * n_gx * tokens.size),
    )(in_hbm(tokens), in_hbm(gain.reshape(1, -1)))


def assemble_kernel(gy_ref, rows_ref, after_ref, out_ref):
    del after_ref
    devices, batch, _ = rows_ref.shape
    quarter = devices // 4
    pack = 16 // batch
    for at, turn in enumerate(ORDER):
        base = (gy_ref[0] ^ turn) * quarter
        for i in range(0, quarter, pack):
            tall = jnp.concatenate(
                [rows_ref[base + i + k].astype(F32) for k in range(pack)], axis=0
            )
            start = (at * quarter + i) * batch
            out_ref[start : start + 16] = tall.astype(BF16)


def assemble(gy, rows, after):
    devices, batch, width = rows.shape
    return pl.pallas_call(
        assemble_kernel,
        in_specs=[SCALARS, WHOLE, ANYWHERE],
        out_specs=WHOLE,
        out_shape=vmem_out((devices * batch, width), BF16),
        compiler_params=params(4),
        cost_estimate=cost(2 * rows.size, 4 * rows.size),
    )(gy, in_vmem(rows), after)


def spread_rows(out_ref, value, gy, columns=slice(None)):
    devices, batch, _ = out_ref.shape
    quarter = devices // 4
    for at, turn in enumerate(ORDER):
        base = (gy ^ turn) * quarter
        for i in range(quarter):
            start = (at * quarter + i) * batch
            out_ref[base + i, :, columns] = value[start : start + batch].astype(out_ref.dtype)


def tie_kernel(*refs):
    del refs


def tie(x, after):
    return pl.pallas_call(
        tie_kernel,
        in_specs=[ANYWHERE] * (1 + len(after)),
        out_specs=ANYWHERE,
        out_shape=jax.ShapeDtypeStruct(x.shape, x.dtype),
        input_output_aliases={0: 0},
        compiler_params=params(1),
        cost_estimate=cost(0, 0),
    )(x, *after)


def in_turn(groups, ahead):
    for group in groups[:ahead]:
        for copy in group:
            copy.start()
    for n, group in enumerate(groups):
        for copy in group:
            copy.wait()
        if n + ahead < len(groups):
            for copy in groups[n + ahead]:
                copy.start()
        yield n


def gate_up_kernel(start, tile, count_after, x_ref, gate_ref, up_ref, *refs):
    keep_ref, send_ref, slots, sems = refs[count_after:]
    _, half, width = keep_ref.shape
    groups = []
    for n in range(width // tile):
        columns = pl.ds(start + n * tile, tile)
        groups.append(
            [
                pltpu.make_async_copy(source.at[:, columns], slots.at[k, n], sems.at[k, n])
                for k, source in enumerate((gate_ref, up_ref))
            ]
        )
    x = x_ref[...]
    for n in in_turn(groups, len(groups)):
        columns = slice(n * tile, (n + 1) * tile)
        for k in range(2):
            value = jnp.dot(x, slots[k, n], preferred_element_type=F32)
            keep_ref[k, :, columns] = value[:half]
            send_ref[k, :, columns] = value[half:].astype(BF16)


def gate_up(x, w_gate, w_up, start, width, after):
    rows, depth = x.shape
    half = rows // 2
    tile = tile_of(width, 256)
    count = width // tile
    return pl.pallas_call(
        functools.partial(gate_up_kernel, start, tile, len(after)),
        in_specs=[WHOLE] + [ANYWHERE] * (2 + len(after)),
        out_specs=[WHOLE, WHOLE],
        out_shape=[vmem_out((2, half, width), F32), vmem_out((2, half, width), BF16)],
        scratch_shapes=[
            pltpu.VMEM((2, count, depth, tile), BF16),
            pltpu.SemaphoreType.DMA((2, count)),
        ],
        compiler_params=params(22),
        cost_estimate=cost(rows * depth * width, depth * width),
    )(in_vmem(x), in_hbm(w_gate), in_hbm(w_up), *after)


def combine_kernel(keep_ref, core_ref, own_ref, across_ref):
    half = own_ref.shape[1]
    own_ref[...] = keep_ref[:, :half] + core_ref[:, :half].astype(F32)
    across_ref[...] = (keep_ref[:, half:] + core_ref[:, half:].astype(F32)).astype(BF16)


def combine(keep, core):
    _, half, width = keep.shape
    shape = (2, half // 2, width)
    return pl.pallas_call(
        combine_kernel,
        in_specs=[WHOLE, WHOLE],
        out_specs=[WHOLE, WHOLE],
        out_shape=[vmem_out(shape, F32), vmem_out(shape, BF16)],
        compiler_params=params(4),
        cost_estimate=cost(keep.size, keep.size),
    )(in_vmem(keep), in_vmem(core))


def activate_kernel(own_ref, far_ref, *refs):
    gate = own_ref[0] + far_ref[0].astype(F32)
    up = own_ref[1] + far_ref[1].astype(F32)
    refs[-1][...] = (jax.nn.silu(gate) * up).astype(BF16)


def activate(own, far, after):
    return pl.pallas_call(
        activate_kernel,
        in_specs=[WHOLE, WHOLE] + [ANYWHERE] * len(after),
        out_specs=WHOLE,
        out_shape=vmem_out(own.shape[1:], BF16),
        compiler_params=params(4),
        cost_estimate=cost(own.size, own.size),
    )(in_vmem(own), in_vmem(far), *after)


def down_kernel(tile, gy_ref, weight_ref, *refs):
    *hidden, out_ref, rows_ref = refs
    start = 0
    for n in range(0, len(hidden), 4):
        depth = hidden[n].shape[1]
        for k, piece in enumerate(hidden[n : n + 4]):
            count = piece.shape[0]
            rows_ref[k * count : (k + 1) * count, start : start + depth] = piece[...]
        start += depth
    gy = gy_ref[0]
    for at in range(0, weight_ref.shape[1], tile):
        columns = slice(at, at + tile)
        value = jnp.dot(rows_ref[...], weight_ref[:, columns], preferred_element_type=F32)
        spread_rows(out_ref, value, gy, columns)


def down(gy, hidden, w_down, devices):
    rows = 4 * hidden[0].shape[0]
    depth, width = w_down.shape
    return pl.pallas_call(
        functools.partial(down_kernel, tile_of(width, 256)),
        in_specs=[SCALARS, WHOLE] + [WHOLE] * len(hidden),
        out_specs=WHOLE,
        out_shape=vmem_out((devices, rows // devices, width), BF16),
        scratch_shapes=[pltpu.VMEM((rows, depth), BF16)],
        compiler_params=params(10),
        cost_estimate=cost(rows * depth * width, depth * width),
    )(gy, in_vmem(w_down), *[in_vmem(h) for h in hidden])


def finish_kernel(tokens_ref, sums_ref, out_ref):
    sources, blocks, _, width = sums_ref.shape
    for b in range(blocks):
        columns = slice(b * width, (b + 1) * width)
        ffn = sums_ref[0, b].astype(F32)
        for s in range(1, sources):
            ffn = ffn + sums_ref[s, b].astype(F32)
        out_ref[:, columns] = (tokens_ref[:, columns].astype(F32) + ffn).astype(BF16)


def finish(tokens, sums):
    return pl.pallas_call(
        finish_kernel,
        in_specs=[WHOLE, WHOLE],
        out_specs=WHOLE,
        out_shape=jax.ShapeDtypeStruct(tokens.shape, BF16),
        compiler_params=params(8),
        cost_estimate=cost(sums.size, 2 * sums.size),
    )(in_vmem(tokens), in_vmem(sums))


def fresh_kernel(gy_ref, x_ref, weight_ref, after_ref, out_ref):
    del after_ref
    value = jnp.dot(x_ref[...], weight_ref[0], preferred_element_type=F32)
    spread_rows(out_ref, value, gy_ref[0])


def fresh_part(gy, x, w_kv, devices, after):
    rows, depth = x.shape
    columns = w_kv.shape[2]
    return pl.pallas_call(
        fresh_kernel,
        in_specs=[SCALARS, WHOLE, WHOLE, ANYWHERE],
        out_specs=WHOLE,
        out_shape=vmem_out((devices, rows // devices, columns), F32),
        compiler_params=params(8),
        cost_estimate=cost(2 * rows * depth * columns, 2 * depth * columns),
    )(gy, in_vmem(x), in_vmem(w_kv), after)


def cache_kernel(
    scale, lengths_ref, query_ref, key_ref, value_ref, after_ref,
    acc_ref, top_ref, sum_ref, keys, values, cache_sems,
):
    del after_ref
    batch = query_ref.shape[0]
    caches = [
        [
            pltpu.make_async_copy(source.at[r], slots.at[r], cache_sems.at[k, r])
            for k, (source, slots) in enumerate(((key_ref, keys), (value_ref, values)))
        ]
        for r in range(batch)
    ]
    for pair in caches:
        for copy in pair:
            copy.start()
    for r in range(batch):
        caches[r][0].wait()
        scores = scale * lax.dot_general(
            query_ref[r], keys[r], (((1,), (1,)), ((), ())), preferred_element_type=F32
        )
        heads = scores.shape[0]
        live = lax.broadcasted_iota(jnp.int32, scores.shape, 1) < lengths_ref[r]
        scores = jnp.where(live, scores, -jnp.inf)
        top = jnp.max(scores, axis=1, keepdims=True)
        chance = jnp.exp(scores - top)
        high = chance.astype(BF16)
        low = (chance - high.astype(F32)).astype(BF16)
        caches[r][1].wait()
        both = jnp.dot(
            jnp.concatenate((high, low), axis=0), values[r], preferred_element_type=F32
        )
        acc_ref[r] = both[:heads] + both[heads:]
        top_ref[r] = top
        sum_ref[r] = jnp.sum(chance, axis=1, keepdims=True)


def attend_cache(grouped, key_cache, value_cache, lengths, after):
    batch, heads, depth = grouped.shape
    span = key_cache.shape[1]
    return pl.pallas_call(
        functools.partial(cache_kernel, 1.0 / math.sqrt(depth)),
        in_specs=[SCALARS, WHOLE] + [ANYWHERE] * 3,
        out_specs=[WHOLE] * 3,
        out_shape=[
            vmem_out((batch, heads, depth), F32),
            vmem_out((batch, heads, 1), F32),
            vmem_out((batch, heads, 1), F32),
        ],
        scratch_shapes=[
            pltpu.VMEM((batch, span, depth), BF16),
            pltpu.VMEM((batch, span, depth), BF16),
            pltpu.SemaphoreType.DMA((2, batch)),
        ],
        compiler_params=params(16),
        cost_estimate=cost(
            6 * batch * heads * span * depth, 4 * batch * span * depth, batch * heads * span
        ),
    )(lengths, in_vmem(grouped), in_hbm(key_cache), in_hbm(value_cache), after)


def attend_new(grouped, cached, key_new, value_new):
    acc, top_cached, sum_cached = cached
    batch = grouped.shape[0]
    scale = 1.0 / math.sqrt(grouped.shape[2])
    own = jnp.einsum("rhd,rd->rh", grouped, key_new, preferred_element_type=F32)
    own = own[:, :, None] * scale
    top = jnp.maximum(top_cached, own)
    old = jnp.exp(top_cached - top)
    new = jnp.exp(own - top)
    total = sum_cached * old + new
    context = (acc * old + new * value_new.astype(F32)[:, None, :]) / total
    return context.astype(BF16).reshape(batch, -1)


def chunk_widths(columns):
    unit = 256 if columns % 256 == 0 else 128
    units = columns // unit
    side = max(1, 5 * units // 18)
    return [unit * u for u in (side, units - 2 * side, side)]


def body(n_gx, n_gy, tokens, gain, w_gate, w_up, w_down, w_kv, queries, key_cache, value_cache, lengths):
    gx = lax.axis_index("gx")
    gy = lax.axis_index("gy").astype(jnp.int32).reshape(1)
    swap_gy = lambda x, bits: swap(x, "gy", n_gy, bits)
    exchange = lambda x: lax.all_to_all(x, ("gx", "gy"), split_axis=0, concat_axis=0, tiled=True)
    devices = n_gx * n_gy
    batch = tokens.shape[0]
    widths = chunk_widths(w_gate.shape[1])

    (normed,) = norm(tokens, gain, n_gx, n_gy, (w_gate.shape[0],))
    gathered = exchange(normed.reshape(devices, batch, -1))
    grouped = queries.reshape(batch, -1, HD)
    cached = attend_cache(grouped, key_cache, value_cache, lengths, normed)
    x = assemble(gy, gathered, cached[0])

    starts = [sum(widths[:c]) for c in range(len(widths))]

    def project(c, after):
        return gate_up(x, w_gate, w_up, starts[c], widths[c], after)

    def back(c, own, after):
        other = tie(swap_gy(own, 2), after)
        return own, other, swap_gy(own, 1), swap_gy(other, 1)

    keep, send = project(0, [])
    slab = w_kv.shape[1]
    part = fresh_part(gy, lax.dynamic_slice_in_dim(x, gx * slab, slab, 1), w_kv, devices, send)
    own_0, across_0 = combine(keep, swap_gy(send, 1))
    far_0 = swap_gy(across_0, 2)
    keep, send = project(1, [across_0])
    hidden_0 = activate(own_0, far_0, [send])
    fresh = jnp.sum(exchange(tie(part, [send])), axis=0)
    key_new = fresh[:, :HD].astype(BF16)
    value_new = fresh[:, HD:].astype(BF16)
    own_1, across_1 = combine(keep, swap_gy(tie(send, [hidden_0]), 1))
    far_1 = swap_gy(across_1, 2)
    keep, send = project(2, [across_1])
    hidden_1 = activate(own_1, far_1, [send])
    pieces_0 = back(0, hidden_0, [send])
    own_2, across_2 = combine(keep, swap_gy(tie(send, [hidden_1, pieces_0[1]]), 1))
    far_2 = swap_gy(across_2, 2)
    hidden_2 = activate(own_2, far_2, [])
    pieces_1 = back(1, tie(hidden_1, [across_2]), [hidden_2])
    pieces_2 = back(2, hidden_2, [])
    total = down(gy, [*pieces_0, *pieces_1, *pieces_2], w_down, devices)

    ffn = exchange(total)
    context = attend_new(grouped, cached, key_new, value_new)
    mixed = finish(tokens, ffn.reshape(n_gx, n_gy, batch, -1))
    return (mixed, context)


def solution(mesh):
    sizes = dict(mesh.shape)
    return jax.shard_map(
        functools.partial(body, sizes["gx"], sizes["gy"]),
        mesh=mesh,
        in_specs=(
            P(("gx", "gy"), None),
            P(),
            P("gy", "gx"),
            P("gy", "gx"),
            P("gx", "gy"),
            P("gy", "gx", None),
            P(("gx", "gy"), None),
            P(("gx", "gy"), None, None),
            P(("gx", "gy"), None, None),
            P(("gx", "gy")),
        ),
        out_specs=(P(("gx", "gy"), None), P(("gx", "gy"), None)),
        check_vma=False,
    )
```

```python
import functools
import math

import jax
import jax.numpy as jnp
from jax import lax
from jax.experimental import pallas as pl
from jax.experimental.pallas import tpu as pltpu
from jax.sharding import PartitionSpec as P

HD = 256
F32 = jnp.float32
BF16 = jnp.bfloat16
MIB = 1024 * 1024
WHOLE = pl.BlockSpec(memory_space=pltpu.VMEM)
SCALARS = pl.BlockSpec(memory_space=pltpu.SMEM)
ANYWHERE = pl.BlockSpec(memory_space=pl.ANY)
ORDER = (0, 2, 1, 3)


def params(mib):
    return pltpu.CompilerParams(vmem_limit_bytes=mib * MIB)


def cost(flops, moved, transcendentals=0):
    return pl.CostEstimate(flops=flops, bytes_accessed=moved, transcendentals=transcendentals)


def tile_of(width, most):
    return max(t for t in range(128, most + 1, 128) if width % t == 0)


def in_hbm(x):
    return pltpu.with_memory_space_constraint(x, pltpu.HBM)


def hbm_out(shape, dtype):
    return pltpu.HBM(shape, dtype)


def vmem_out(shape, dtype):
    return pltpu.VMEM(shape, dtype)


def in_vmem(x):
    return pltpu.with_memory_space_constraint(x, pltpu.VMEM)


def swap(x, axis, size, bits):
    return lax.ppermute(x, axis, [(i, i ^ bits) for i in range(size)])


def norm_kernel(tokens_hbm, gain_hbm, *refs):
    *out_refs, tokens_ref, gain_ref, sems = refs
    copies, blocks = out_refs[0].shape[:2]
    width = sum(ref.shape[3] for ref in out_refs)
    moves = [
        pltpu.make_async_copy(source, target, sems.at[k])
        for k, (source, target) in enumerate(((tokens_hbm, tokens_ref), (gain_hbm, gain_ref)))
    ]
    for move in moves:
        move.start()
    for move in moves:
        move.wait()
    values = tokens_ref[...].astype(F32)
    centred = values - jnp.mean(values, axis=-1, keepdims=True)
    spread = jnp.mean(centred * centred, axis=-1, keepdims=True)
    normed = (centred * lax.rsqrt(spread + 1e-05) * gain_ref[...]).astype(BF16)
    for b in range(blocks):
        start = b * width
        for out_ref in out_refs:
            part = normed[:, start : start + out_ref.shape[3]]
            start += out_ref.shape[3]
            for c in range(copies):
                out_ref[c, b] = part


def norm(tokens, gain, n_gx, n_gy, widths):
    batch, channels = tokens.shape
    return pl.pallas_call(
        norm_kernel,
        in_specs=[ANYWHERE, ANYWHERE],
        out_specs=[WHOLE] * len(widths),
        out_shape=[vmem_out((n_gx, n_gy, batch, width), BF16) for width in widths],
        scratch_shapes=[
            pltpu.VMEM((batch, channels), BF16),
            pltpu.VMEM((1, channels), F32),
            pltpu.SemaphoreType.DMA((2,)),
        ],
        compiler_params=params(8),
        cost_estimate=cost(10 * tokens.size, 2 * n_gx * tokens.size),
    )(in_hbm(tokens), in_hbm(gain.reshape(1, -1)))


def assemble_kernel(gy_ref, rows_ref, after_ref, out_ref):
    del after_ref
    devices, batch, _ = rows_ref.shape
    quarter = devices // 4
    pack = 16 // batch
    for at, turn in enumerate(ORDER):
        base = (gy_ref[0] ^ turn) * quarter
        for i in range(0, quarter, pack):
            tall = jnp.concatenate(
                [rows_ref[base + i + k].astype(F32) for k in range(pack)], axis=0
            )
            start = (at * quarter + i) * batch
            out_ref[start : start + 16] = tall.astype(BF16)


def assemble(gy, rows, after):
    devices, batch, width = rows.shape
    return pl.pallas_call(
        assemble_kernel,
        in_specs=[SCALARS, WHOLE, ANYWHERE],
        out_specs=WHOLE,
        out_shape=vmem_out((devices * batch, width), BF16),
        compiler_params=params(4),
        cost_estimate=cost(2 * rows.size, 4 * rows.size),
    )(gy, in_vmem(rows), after)


def spread_rows(out_ref, value, gy, columns=slice(None)):
    devices, batch, _ = out_ref.shape
    quarter = devices // 4
    for at, turn in enumerate(ORDER):
        base = (gy ^ turn) * quarter
        for i in range(quarter):
            start = (at * quarter + i) * batch
            out_ref[base + i, :, columns] = value[start : start + batch].astype(out_ref.dtype)


def tie_kernel(*refs):
    del refs


def tie(x, after):
    return pl.pallas_call(
        tie_kernel,
        in_specs=[ANYWHERE] * (1 + len(after)),
        out_specs=ANYWHERE,
        out_shape=jax.ShapeDtypeStruct(x.shape, x.dtype),
        input_output_aliases={0: 0},
        compiler_params=params(1),
        cost_estimate=cost(0, 0),
    )(x, *after)


def in_turn(groups, ahead):
    for group in groups[:ahead]:
        for copy in group:
            copy.start()
    for n, group in enumerate(groups):
        for copy in group:
            copy.wait()
        if n + ahead < len(groups):
            for copy in groups[n + ahead]:
                copy.start()
        yield n


def gate_up_kernel(start, tile, count_after, x_ref, gate_ref, up_ref, *refs):
    keep_ref, send_ref, slots, sems = refs[count_after:]
    _, half, width = keep_ref.shape
    groups = []
    for n in range(width // tile):
        columns = pl.ds(start + n * tile, tile)
        groups.append(
            [
                pltpu.make_async_copy(source.at[:, columns], slots.at[k, n], sems.at[k, n])
                for k, source in enumerate((gate_ref, up_ref))
            ]
        )
    x = x_ref[...]
    for n in in_turn(groups, len(groups)):
        columns = slice(n * tile, (n + 1) * tile)
        for k in range(2):
            value = jnp.dot(x, slots[k, n], preferred_element_type=F32)
            keep_ref[k, :, columns] = value[:half]
            send_ref[k, :, columns] = value[half:].astype(BF16)


def gate_up(x, w_gate, w_up, start, width, after):
    rows, depth = x.shape
    half = rows // 2
    tile = tile_of(width, 256)
    count = width // tile
    return pl.pallas_call(
        functools.partial(gate_up_kernel, start, tile, len(after)),
        in_specs=[WHOLE] + [ANYWHERE] * (2 + len(after)),
        out_specs=[WHOLE, WHOLE],
        out_shape=[vmem_out((2, half, width), F32), vmem_out((2, half, width), BF16)],
        scratch_shapes=[
            pltpu.VMEM((2, count, depth, tile), BF16),
            pltpu.SemaphoreType.DMA((2, count)),
        ],
        compiler_params=params(22),
        cost_estimate=cost(rows * depth * width, depth * width),
    )(in_vmem(x), in_hbm(w_gate), in_hbm(w_up), *after)


def combine_kernel(keep_ref, core_ref, own_ref, across_ref):
    half = own_ref.shape[1]
    own_ref[...] = keep_ref[:, :half] + core_ref[:, :half].astype(F32)
    across_ref[...] = (keep_ref[:, half:] + core_ref[:, half:].astype(F32)).astype(BF16)


def combine(keep, core):
    _, half, width = keep.shape
    shape = (2, half // 2, width)
    return pl.pallas_call(
        combine_kernel,
        in_specs=[WHOLE, WHOLE],
        out_specs=[WHOLE, WHOLE],
        out_shape=[vmem_out(shape, F32), vmem_out(shape, BF16)],
        compiler_params=params(4),
        cost_estimate=cost(keep.size, keep.size),
    )(in_vmem(keep), in_vmem(core))


def activate_kernel(own_ref, far_ref, *refs):
    gate = own_ref[0] + far_ref[0].astype(F32)
    up = own_ref[1] + far_ref[1].astype(F32)
    refs[-1][...] = (jax.nn.silu(gate) * up).astype(BF16)


def activate(own, far, after):
    return pl.pallas_call(
        activate_kernel,
        in_specs=[WHOLE, WHOLE] + [ANYWHERE] * len(after),
        out_specs=WHOLE,
        out_shape=vmem_out(own.shape[1:], BF16),
        compiler_params=params(4),
        cost_estimate=cost(own.size, own.size),
    )(in_vmem(own), in_vmem(far), *after)


def down_kernel(start, tile, has_sum, last, gy_ref, *refs):
    hidden, (weight_ref, *refs) = refs[:4], refs[4:]
    sum_ref = refs.pop(0) if has_sum else None
    out_ref, slots, sems = refs[-3:]
    depth = hidden[0].shape[1]
    width = weight_ref.shape[1]
    groups = [
        [
            pltpu.make_async_copy(
                weight_ref.at[pl.ds(start, depth), pl.ds(n * tile, tile)],
                slots.at[n],
                sems.at[n],
            )
        ]
        for n in range(width // tile)
    ]
    x = jnp.concatenate([h[...] for h in hidden], axis=0)
    gy = gy_ref[0]
    for n in in_turn(groups, len(groups)):
        columns = slice(n * tile, (n + 1) * tile)
        value = jnp.dot(x, slots[n], preferred_element_type=F32)
        if has_sum:
            value = value + sum_ref[:, columns]
        if last:
            spread_rows(out_ref, value, gy, columns)
        else:
            out_ref[:, columns] = value


def down(gy, hidden, w_down, start, total, devices, last, after):
    part_rows, depth = hidden[0].shape
    rows = 4 * part_rows
    width = w_down.shape[1]
    tile = tile_of(width, 256)
    count = width // tile
    args = [gy, *[in_vmem(h) for h in hidden], in_hbm(w_down)]
    in_specs = [SCALARS] + [WHOLE] * 4 + [ANYWHERE]
    if total is not None:
        args.append(in_vmem(total))
        in_specs.append(WHOLE)
    args.extend(after)
    in_specs.extend([ANYWHERE] * len(after))
    shape = (devices, rows // devices, width) if last else (rows, width)
    return pl.pallas_call(
        functools.partial(down_kernel, start, tile, total is not None, last),
        in_specs=in_specs,
        out_specs=WHOLE,
        out_shape=vmem_out(shape, BF16 if last else F32),
        scratch_shapes=[
            pltpu.VMEM((count, depth, tile), BF16),
            pltpu.SemaphoreType.DMA((count,)),
        ],
        compiler_params=params(22),
        cost_estimate=cost(rows * depth * width, depth * width),
    )(*args)


def finish_kernel(tokens_ref, sums_ref, out_ref):
    sources, blocks, _, width = sums_ref.shape
    for b in range(blocks):
        columns = slice(b * width, (b + 1) * width)
        ffn = sums_ref[0, b].astype(F32)
        for s in range(1, sources):
            ffn = ffn + sums_ref[s, b].astype(F32)
        out_ref[:, columns] = (tokens_ref[:, columns].astype(F32) + ffn).astype(BF16)


def finish(tokens, sums):
    return pl.pallas_call(
        finish_kernel,
        in_specs=[WHOLE, WHOLE],
        out_specs=WHOLE,
        out_shape=jax.ShapeDtypeStruct(tokens.shape, BF16),
        compiler_params=params(8),
        cost_estimate=cost(sums.size, 2 * sums.size),
    )(in_vmem(tokens), in_vmem(sums))


def fresh_kernel(gy_ref, x_ref, weight_ref, after_ref, out_ref):
    del after_ref
    value = jnp.dot(x_ref[...], weight_ref[0], preferred_element_type=F32)
    spread_rows(out_ref, value, gy_ref[0])


def fresh_part(gy, x, w_kv, devices, after):
    rows, depth = x.shape
    columns = w_kv.shape[2]
    return pl.pallas_call(
        fresh_kernel,
        in_specs=[SCALARS, WHOLE, WHOLE, ANYWHERE],
        out_specs=WHOLE,
        out_shape=vmem_out((devices, rows // devices, columns), F32),
        compiler_params=params(8),
        cost_estimate=cost(2 * rows * depth * columns, 2 * depth * columns),
    )(gy, in_vmem(x), in_vmem(w_kv), after)


def cache_kernel(
    scale, lengths_ref, query_ref, key_ref, value_ref, after_ref,
    acc_ref, top_ref, sum_ref, keys, values, cache_sems,
):
    del after_ref
    batch = query_ref.shape[0]
    caches = [
        [
            pltpu.make_async_copy(source.at[r], slots.at[r], cache_sems.at[k, r])
            for k, (source, slots) in enumerate(((key_ref, keys), (value_ref, values)))
        ]
        for r in range(batch)
    ]
    for pair in caches:
        for copy in pair:
            copy.start()
    for r in range(batch):
        caches[r][0].wait()
        scores = scale * lax.dot_general(
            query_ref[r], keys[r], (((1,), (1,)), ((), ())), preferred_element_type=F32
        )
        heads = scores.shape[0]
        live = lax.broadcasted_iota(jnp.int32, scores.shape, 1) < lengths_ref[r]
        scores = jnp.where(live, scores, -jnp.inf)
        top = jnp.max(scores, axis=1, keepdims=True)
        chance = jnp.exp(scores - top)
        high = chance.astype(BF16)
        low = (chance - high.astype(F32)).astype(BF16)
        caches[r][1].wait()
        both = jnp.dot(
            jnp.concatenate((high, low), axis=0), values[r], preferred_element_type=F32
        )
        acc_ref[r] = both[:heads] + both[heads:]
        top_ref[r] = top
        sum_ref[r] = jnp.sum(chance, axis=1, keepdims=True)


def attend_cache(grouped, key_cache, value_cache, lengths, after):
    batch, heads, depth = grouped.shape
    span = key_cache.shape[1]
    return pl.pallas_call(
        functools.partial(cache_kernel, 1.0 / math.sqrt(depth)),
        in_specs=[SCALARS, WHOLE] + [ANYWHERE] * 3,
        out_specs=[WHOLE] * 3,
        out_shape=[
            vmem_out((batch, heads, depth), F32),
            vmem_out((batch, heads, 1), F32),
            vmem_out((batch, heads, 1), F32),
        ],
        scratch_shapes=[
            pltpu.VMEM((batch, span, depth), BF16),
            pltpu.VMEM((batch, span, depth), BF16),
            pltpu.SemaphoreType.DMA((2, batch)),
        ],
        compiler_params=params(16),
        cost_estimate=cost(
            6 * batch * heads * span * depth, 4 * batch * span * depth, batch * heads * span
        ),
    )(lengths, in_vmem(grouped), in_hbm(key_cache), in_hbm(value_cache), after)


def attend_new(grouped, cached, key_new, value_new):
    acc, top_cached, sum_cached = cached
    batch = grouped.shape[0]
    scale = 1.0 / math.sqrt(grouped.shape[2])
    own = jnp.einsum("rhd,rd->rh", grouped, key_new, preferred_element_type=F32)
    own = own[:, :, None] * scale
    top = jnp.maximum(top_cached, own)
    old = jnp.exp(top_cached - top)
    new = jnp.exp(own - top)
    total = sum_cached * old + new
    context = (acc * old + new * value_new.astype(F32)[:, None, :]) / total
    return context.astype(BF16).reshape(batch, -1)


def chunk_widths(columns):
    unit = 256 if columns % 256 == 0 else 128
    units = columns // unit
    side = max(1, 5 * units // 18)
    return [unit * u for u in (side, units - 2 * side, side)]


def body(n_gx, n_gy, tokens, gain, w_gate, w_up, w_down, w_kv, queries, key_cache, value_cache, lengths):
    gx = lax.axis_index("gx")
    gy = lax.axis_index("gy").astype(jnp.int32).reshape(1)
    swap_gy = lambda x, bits: swap(x, "gy", n_gy, bits)
    exchange = lambda x: lax.all_to_all(x, ("gx", "gy"), split_axis=0, concat_axis=0, tiled=True)
    devices = n_gx * n_gy
    batch = tokens.shape[0]
    widths = chunk_widths(w_gate.shape[1])

    (normed,) = norm(tokens, gain, n_gx, n_gy, (w_gate.shape[0],))
    gathered = exchange(normed.reshape(devices, batch, -1))
    grouped = queries.reshape(batch, -1, HD)
    cached = attend_cache(grouped, key_cache, value_cache, lengths, normed)
    x = assemble(gy, gathered, cached[0])

    starts = [sum(widths[:c]) for c in range(len(widths))]

    def project(c, after):
        return gate_up(x, w_gate, w_up, starts[c], widths[c], after)

    def back(c, own, after):
        other = tie(swap_gy(own, 2), after)
        return own, other, swap_gy(own, 1), swap_gy(other, 1)

    def through(c, pieces, total, after):
        last = c == len(widths) - 1
        return down(gy, pieces, w_down, starts[c], total, devices, last, after)

    keep, send = project(0, [])
    slab = w_kv.shape[1]
    part = fresh_part(gy, lax.dynamic_slice_in_dim(x, gx * slab, slab, 1), w_kv, devices, send)
    own_0, across_0 = combine(keep, swap_gy(send, 1))
    far_0 = swap_gy(across_0, 2)
    keep, send = project(1, [across_0])
    hidden_0 = activate(own_0, far_0, [send])
    fresh = jnp.sum(exchange(tie(part, [send])), axis=0)
    key_new = fresh[:, :HD].astype(BF16)
    value_new = fresh[:, HD:].astype(BF16)
    own_1, across_1 = combine(keep, swap_gy(tie(send, [hidden_0]), 1))
    far_1 = swap_gy(across_1, 2)
    keep, send = project(2, [across_1])
    hidden_1 = activate(own_1, far_1, [send])
    pieces_0 = back(0, hidden_0, [send])
    own_2, across_2 = combine(keep, swap_gy(tie(send, [hidden_1, pieces_0[1]]), 1))
    far_2 = swap_gy(across_2, 2)
    total = through(0, pieces_0, None, [across_2])
    pieces_1 = back(1, hidden_1, [across_2])
    total = through(1, pieces_1, total, [])
    hidden_2 = activate(own_2, far_2, [total])
    pieces_2 = back(2, hidden_2, [])
    total = through(2, pieces_2, total, [])

    ffn = exchange(total)
    context = attend_new(grouped, cached, key_new, value_new)
    mixed = finish(tokens, ffn.reshape(n_gx, n_gy, batch, -1))
    return (mixed, context)


def solution(mesh):
    sizes = dict(mesh.shape)
    return jax.shard_map(
        functools.partial(body, sizes["gx"], sizes["gy"]),
        mesh=mesh,
        in_specs=(
            P(("gx", "gy"), None),
            P(),
            P("gy", "gx"),
            P("gy", "gx"),
            P("gx", "gy"),
            P("gy", "gx", None),
            P(("gx", "gy"), None),
            P(("gx", "gy"), None, None),
            P(("gx", "gy"), None, None),
            P(("gx", "gy")),
        ),
        out_specs=(P(("gx", "gy"), None), P(("gx", "gy"), None)),
        check_vma=False,
    )
```
